128 devices in a mesh: vox: 8 (over x, core), var: 16 (over y, z).
Axes of the slice: x: 4, y: 4, z: 4, core: 2. Of those that a mesh axis runs over, the one named last changes fastest.
Arguments:
- cross: float32 [16384, 24576], P('vox', 'var')
- start: float32 [32, 24576], P(None, 'var'), may hold values from -6 to 6
- levels: int32 [2, 32], replicated, may hold values from 0 to 767, as said below
Outputs:
- deflated: float32 [16384, 24576], P('vox', 'var')
- left_dirs: float32 [32, 16384], P(None, 'vox')
- right_dirs: float32 [32, 24576], P(None, 'var')
- strength: float32 [32], replicated
The draws below stay inside these ranges and needn't reach their ends.
Inputs may be any that keep to these rules, and one draw needn't show every extreme that they name: `levels`: both 0 and 767 occur in every draw.
All inputs are finite; a program needn't handle non-finite values.
Results may differ from the reference program's by a relative error of at most 0.0003.
Values sent between devices are 32-bit elements; how exact they have to be, the bound alone decides.
No kernel may reach another device: no remote copies, remote signals or barrier semaphores. Data moves between devices by JAX's collectives and lax.ppermute only.
A program may use at most 128 MiB of HBM per device.

```python
import math
import jax
import jax.numpy as jnp
from jax import lax

NV = 16384
NG = 24576
K = 32
ITERS = 2


def draw_cross(key, part):
    keys = jax.random.split(jax.random.fold_in(key, 7), 3)
    ramp_rows = 1.0 + 2.0 * jnp.arange(NV, dtype=jnp.float32) / NV
    ramp_cols = 1.0 + 2.0 * jnp.arange(NG, dtype=jnp.float32) / NG
    row_scale = jnp.exp(jax.random.uniform(keys[0], (NV,), jnp.float32, 0.0, math.log(10.0))) * ramp_rows / 5.0
    col_scale = jnp.exp(jax.random.uniform(keys[1], (NG,), jnp.float32, 0.0, math.log(10.0))) * ramp_cols / 5.0
    noise = jax.random.normal(keys[2], (NV, NG), jnp.float32)
    return noise * row_scale[:, None] * col_scale[None, :]


def draw_levels(key, part):
    keys = jax.random.split(jax.random.fold_in(key, 11), 3)
    values = jax.random.randint(keys[0], (2 * K,), 0, 768)
    high_pos = jax.random.randint(keys[1], (), 0, 2 * K)
    low_pos = (high_pos + 1 + jax.random.randint(keys[2], (), 0, 2 * K - 1)) % (2 * K)
    where_idx = jnp.arange(2 * K)
    values = jnp.where(where_idx == high_pos, 767, values)
    values = jnp.where(where_idx == low_pos, 0, values)
    return values.reshape(2, K).astype(jnp.int32)


def steps_of(stream_key, extent, cuts, smallest, high):
    def one(axis_at, shards_of):
        draws = jax.random.uniform(jax.random.fold_in(jax.random.fold_in(stream_key, 6), axis_at), (shards_of,), jnp.float32, smallest / len(cuts), high / len(cuts))
        return jnp.repeat(jnp.exp(draws), extent[axis_at] // shards_of).reshape((-1,) + (1,) * (len(extent) - axis_at - 1))

    level = one(*cuts[0])
    for cut in cuts[1:]:
        level = level * one(*cut)
    return level


def normal_values(own_key, shape, deviation, bound, cuts=(), held_as=jnp.bfloat16):
    result = deviation * jax.random.normal(own_key, shape, jnp.float32)
    if cuts:
        result = result * steps_of(own_key, shape, cuts, -0.22, 0.18)
    return jnp.clip(result, -bound, bound).astype(held_as)


def setup_inputs(seed: int = 0) -> dict:
    arg_keys = jax.random.split(jax.random.key(seed), 4)
    cross = draw_cross(jax.random.fold_in(arg_keys[3], 71), 0)
    start = normal_values(arg_keys[1], (K, NG), 1.0, 6.0, ((1, 16),), jnp.float32)
    levels = draw_levels(jax.random.fold_in(arg_keys[3], 71), 0)
    return dict(cross=cross, start=start, levels=levels)


EPSILON = 1e-06
HIGH = lax.Precision.HIGHEST

def shrink(values, thresholds, mean_sq):
    level = (thresholds * jnp.sqrt(mean_sq + EPSILON))[:, None]
    return values - jnp.clip(values, -level, level)

def orthonormal(shrunk, count):
    gram = lax.dot_general(shrunk.astype(jnp.float32), shrunk.astype(jnp.float32), (((1,), (1,)), ((), ())), precision=HIGH, preferred_element_type=jnp.float32)
    gram = gram / count + EPSILON * jnp.eye(gram.shape[0], dtype=jnp.float32)
    factor = jnp.linalg.cholesky(gram)
    return jax.scipy.linalg.solve_triangular(factor, shrunk, lower=True)

def reference(cross, start, levels):
    thresholds = levels.astype(jnp.float32) / 1024.0
    right_dirs = start
    left_dirs = None
    for sweep in range(ITERS):
        summed = lax.dot_general(right_dirs.astype(jnp.float32), cross.astype(jnp.float32), (((1,), (1,)), ((), ())), precision=HIGH, preferred_element_type=jnp.float32)
        shrunk = shrink(summed, thresholds[0], lax.optimization_barrier(jnp.sum(summed * summed, 1)) / NV)
        left_dirs = orthonormal(shrunk, NV)
        summed = jnp.dot(left_dirs.astype(jnp.float32), cross.astype(jnp.float32), precision=HIGH, preferred_element_type=jnp.float32)
        shrunk = shrink(summed, thresholds[1], lax.optimization_barrier(jnp.sum(summed * summed, 1)) / NG)
        right_dirs = orthonormal(shrunk, NG)
    projected = lax.dot_general(right_dirs.astype(jnp.float32), cross.astype(jnp.float32), (((1,), (1,)), ((), ())), precision=HIGH, preferred_element_type=jnp.float32)
    strength = lax.optimization_barrier(jnp.sum(left_dirs * projected, 1)) / math.sqrt(NV * NG)
    scaled = left_dirs * (strength / math.sqrt(NV * NG))[:, None]
    block_size = math.gcd(NV, 1024)
    nblocks = NV // block_size
    cross_blocks = cross.reshape(nblocks, block_size, NG)
    scaled_blocks = scaled.reshape(K, nblocks, block_size).transpose(1, 0, 2)

    def deflate_block(pair):
        block_rows, block_scaled = pair
        removed = lax.dot_general(block_scaled.astype(jnp.float32), right_dirs.astype(jnp.float32), (((0,), (0,)), ((), ())), precision=HIGH, preferred_element_type=jnp.float32)
        return block_rows - removed
    deflated = lax.map(deflate_block, (cross_blocks, scaled_blocks)).reshape(NV, NG)
    return (deflated, left_dirs, right_dirs, strength)
```

```python
import math

import jax
import jax.numpy as jnp
from jax import lax
from jax.sharding import PartitionSpec as P

NV = 16384
NG = 24576
K = 32
ITERS = 2

EPSILON = 1e-06
HIGHEST = lax.Precision.HIGHEST
HIGH = lax.Precision.HIGH

X_RINGS = [[x * 2 + c for x in range(4)] for c in range(2)]
CORE_PAIRS = [[x * 2, x * 2 + 1] for x in range(4)]
Y_RINGS = [[y * 4 + z for y in range(4)] for z in range(4)]
Z_RINGS = [[y * 4 + z for z in range(4)] for y in range(4)]


def shift(value, axis, rings, step):
    pairs = [(r[i], r[(i + step) % len(r)]) for r in rings for i in range(len(r))]
    return lax.ppermute(value, axis, pairs)


def ring_sum(value, axis, rings):
    got = [shift(value, axis, rings, step) for step in (1, 3, 2)]
    return (value + got[0]) + (got[1] + got[2])


def pair_sum(value):
    return value + shift(value, "vox", CORE_PAIRS, 1)


def shrink(values, thresholds, mean_sq):
    level = (thresholds * jnp.sqrt(mean_sq + EPSILON))[:, None]
    return values - jnp.clip(values, -level, level)


def small_gram(a, b):
    return lax.dot_general(
        a, b, (((1,), (1,)), ((), ())), precision=HIGHEST, preferred_element_type=jnp.float32
    )


def inverse_factor(gram, count):
    gram = gram / count + EPSILON * jnp.eye(K, dtype=jnp.float32)
    factor = jnp.linalg.cholesky(gram)
    return jax.scipy.linalg.solve_triangular(factor, jnp.eye(K, dtype=jnp.float32), lower=True)


def mix(matrix, values):
    return jnp.dot(matrix, values, precision=HIGHEST, preferred_element_type=jnp.float32)


def left_sum_of(cross, right, gram_part, z):
    part = lax.dot_general(
        right, cross, (((1,), (1,)), ((), ())), precision=HIGH, preferred_element_type=jnp.float32
    )
    width = part.shape[1] // 4

    def piece(step):
        block = lax.dynamic_slice(part, (0, ((z + step) % 4) * width), (K, width))
        if gram_part is None:
            return block
        return jnp.concatenate([block, gram_part], axis=1)

    total = piece(0)
    for step in (1, 3, 2):
        total = total + shift(piece(step), "var", Z_RINGS, step)
    total = ring_sum(total, "var", Y_RINGS)
    block = total[:, :width]
    full = jnp.zeros_like(part)
    full = lax.dynamic_update_slice(full, block, (0, z * width))
    for step in (1, 3, 2):
        got = shift(block, "var", Z_RINGS, step)
        full = lax.dynamic_update_slice(full, got, (0, ((z - step) % 4) * width))
    if gram_part is None:
        return full, None
    inverse = inverse_factor(total[:, width:], NG)
    return mix(inverse, full), inverse


def right_sum_of(cross, left, gram_part, core):
    part = jnp.dot(left, cross, precision=HIGH, preferred_element_type=jnp.float32)
    width = part.shape[1] // 2

    def piece(step):
        block = lax.dynamic_slice(part, (0, ((core + step) % 2) * width), (K, width))
        return jnp.concatenate([block, gram_part], axis=1)

    total = piece(0) + shift(piece(1), "vox", CORE_PAIRS, 1)
    total = ring_sum(total, "vox", X_RINGS)
    block = total[:, :width]
    got = shift(block, "vox", CORE_PAIRS, 1)
    full = jnp.where(
        core == 0, jnp.concatenate([block, got], axis=1), jnp.concatenate([got, block], axis=1)
    )
    inverse = inverse_factor(total[:, width:], NV)
    return mix(inverse, full), inverse


def per_device(cross, start, levels):
    core = lax.axis_index("vox") % 2
    z = lax.axis_index("var") % 4
    thresholds = levels.astype(jnp.float32) / 1024.0
    right = start
    gram_right = None
    for sweep in range(ITERS):
        left_sum, _ = left_sum_of(cross, right, gram_right, z)
        squares = jnp.sum(left_sum * left_sum, 1)
        squares = ring_sum(pair_sum(squares), "vox", X_RINGS)
        left = shrink(left_sum, thresholds[0], squares / NV)
        right_sum, left_inverse = right_sum_of(cross, left, small_gram(left, left), core)
        squares = jnp.sum(right_sum * right_sum, 1)
        squares = ring_sum(ring_sum(squares, "var", Y_RINGS), "var", Z_RINGS)
        right = shrink(right_sum, thresholds[1], squares / NG)
        gram_right = small_gram(right, right)
    left_dirs = mix(left_inverse, left)
    last = jnp.concatenate([gram_right, small_gram(right_sum, right)], axis=1)
    last = ring_sum(ring_sum(last, "var", Y_RINGS), "var", Z_RINGS)
    right_inverse = inverse_factor(last[:, :K], NG)
    right_dirs = mix(right_inverse, right)
    strength = jnp.sum(right_inverse * last[:, K:], 1) / math.sqrt(NV * NG)
    scaled = left_dirs * (strength / math.sqrt(NV * NG))[:, None]
    removed = lax.dot_general(
        scaled,
        right_dirs,
        (((0,), (0,)), ((), ())),
        precision=HIGHEST,
        preferred_element_type=jnp.float32,
    )
    deflated = cross - removed
    return (deflated, left_dirs, right_dirs, strength)


def solution(mesh):
    in_specs = (P("vox", "var"), P(None, "var"), P())
    out_specs = (P("vox", "var"), P(None, "vox"), P(None, "var"), P())
    return jax.shard_map(
        per_device, mesh=mesh, in_specs=in_specs, out_specs=out_specs, check_vma=False
    )
```

```python
import math

import jax
import jax.numpy as jnp
from jax import lax
from jax.experimental import pallas as pl
from jax.experimental.pallas import tpu as pltpu
from jax.sharding import PartitionSpec as P

NV = 16384
NG = 24576
K = 32
ITERS = 2
ROWS = 2048
COLS = 1536
QUARTER = ROWS // 4
HALF = COLS // 2
BLOCK = 512
LANES = 128

EPSILON = 1e-06
HIGHEST = lax.Precision.HIGHEST
F32 = jnp.float32
BF16 = jnp.bfloat16
NT = (((1,), (1,)), ((), ()))
NN = (((1,), (0,)), ((), ()))
TN = (((0,), (0,)), ((), ()))

X_RINGS = [[x * 2 + c for x in range(4)] for c in range(2)]
CORE_PAIRS = [[x * 2, x * 2 + 1] for x in range(4)]
Y_RINGS = [[y * 4 + z for y in range(4)] for z in range(4)]
Z_RINGS = [[y * 4 + z for z in range(4)] for y in range(4)]
STEPS = (1, 3, 2)

PARAMS = pltpu.CompilerParams(vmem_limit_bytes=40 * 2**20)


def shift(value, axis, rings, step):
    pairs = [(r[i], r[(i + step) % len(r)]) for r in rings for i in range(len(r))]
    return lax.ppermute(value, axis, pairs)


def ring_sum(value, axis, rings):
    got = [shift(value, axis, rings, step) for step in STEPS]
    return (value + got[0]) + (got[1] + got[2])


def pair_sum(value):
    return value + shift(value, "vox", CORE_PAIRS, 1)


def dot(a, b, dims):
    return lax.dot_general(a, b, dims, preferred_element_type=F32)


def full_dot(a, b, dims):
    return lax.dot_general(a, b, dims, precision=HIGHEST, preferred_element_type=F32)


def split2(x):
    high = x.astype(BF16)
    return high, (x - high.astype(F32)).astype(BF16)


def split3(x):
    high = x.astype(BF16)
    rest = x - high.astype(F32)
    middle = rest.astype(BF16)
    return high, middle, (rest - middle.astype(F32)).astype(BF16)


def diagonal(width=LANES, offset=0):
    row = lax.broadcasted_iota(jnp.int32, (K, width), 0)
    lane = lax.broadcasted_iota(jnp.int32, (K, width), 1)
    return lane == row + offset


def to_column(row):
    return jnp.sum(jnp.where(diagonal(K), row, 0.0), axis=1, keepdims=True)


def to_row(column):
    return jnp.sum(jnp.where(diagonal(), column, 0.0), axis=0, keepdims=True)


def cross_gram(a, b):
    parts = dot(jnp.concatenate(split3(a), axis=0), jnp.concatenate(split3(b), axis=0), NT)
    rows = parts[:K] + (parts[K : 2 * K] + parts[2 * K :])
    return rows[:, :K] + (rows[:, K : 2 * K] + rows[:, 2 * K :])


def shrunk_of(values, squares, levels, side, count):
    thresholds = levels[side : side + 1, :].astype(F32) / 1024.0
    level = to_column(thresholds * jnp.sqrt(squares[:, :K] / count + EPSILON))
    return values - jnp.clip(values, -level, level)


def padded(small):
    return jnp.concatenate([small, jnp.zeros((K, LANES - small.shape[1]), F32)], axis=1)


def inverse_factor(gram, count):
    start = gram / count + jnp.where(diagonal(K), EPSILON, 0.0)
    start = jnp.concatenate(
        [jnp.where(diagonal(K), 1.0, 0.0), start, jnp.zeros((K, LANES - 2 * K), F32)], axis=1
    )
    blocks = [start[8 * b : 8 * b + 8] for b in range(4)]
    row = lax.broadcasted_iota(jnp.int32, (8, LANES), 0)
    pivots = []
    for panel in range(4):
        columns = [
            {
                b: jnp.broadcast_to(blocks[b][:, K + 8 * panel + t : K + 8 * panel + t + 1], (8, LANES))
                for b in range(panel, 4)
            }
            for t in range(8)
        ]
        pivot_of = jnp.ones((8, LANES), F32)
        for t in range(8):
            pivot = columns[t][panel][t : t + 1]
            pivot_of = jnp.where(row == t, pivot, pivot_of)
            inverse = 1.0 / pivot
            top = blocks[panel][t : t + 1]
            for b in range(panel, 4):
                factor = columns[t][b] * inverse
                if b == panel:
                    factor = jnp.where(row > t, factor, 0.0)
                columns[t][b] = factor
            for u in range(t + 1, 8):
                head = columns[u][panel][t : t + 1]
                for b in range(panel, 4):
                    columns[u][b] = columns[u][b] - columns[t][b] * head
            for b in range(panel, 4):
                blocks[b] = blocks[b] - columns[t][b] * top
        pivots.append(pivot_of)
    scale = 1.0 / jnp.sqrt(jnp.concatenate(pivots, axis=0))
    return (jnp.concatenate(blocks, axis=0) * scale)[:, :K]


def left_product(right, squares, levels, cross, z):
    first = squares is None
    width = QUARTER if first else QUARTER + LANES

    def kernel(z_ref, *refs):
        if first:
            right_ref, cross_ref, *outs, both_ref = refs
        else:
            right_ref, squares_ref, levels_ref, cross_ref, *outs, both_ref, gram_ref = refs
        step = pl.program_id(0)

        @pl.when(step == 0)
        def _():
            values = right_ref[...]
            if not first:
                values = shrunk_of(values, squares_ref[...], levels_ref[...], 1, NG)
                gram_ref[...] = padded(cross_gram(values, values))
            both_ref[...] = jnp.concatenate(split2(values), axis=0)

        high, low = split2(cross_ref[...])
        whole = dot(both_ref[...], high, NT)
        product = whole[:K] + (whole[K:] + dot(both_ref[:K], low, NT))
        for at in range(4):

            @pl.when(step == at)
            def _():
                outs[at][:, :QUARTER] = product
                if not first:
                    outs[at][:, QUARTER:] = gram_ref[...]

    small = [] if first else [
        pl.BlockSpec((1, LANES), lambda i, z: (0, 0)),
        pl.BlockSpec((2, K), lambda i, z: (0, 0)),
    ]
    scratch = [pltpu.VMEM((2 * K, COLS), BF16)]
    if not first:
        scratch.append(pltpu.VMEM((K, LANES), F32))
    args = (right,) if first else (right, squares, levels)
    return pl.pallas_call(
        kernel,
        grid_spec=pltpu.PrefetchScalarGridSpec(
            num_scalar_prefetch=1,
            grid=(4,),
            in_specs=[pl.BlockSpec((K, COLS), lambda i, z: (0, 0))]
            + small
            + [pl.BlockSpec((QUARTER, COLS), lambda i, z: (lax.rem(z[0] + i, 4), 0))],
            out_specs=[pl.BlockSpec((K, width), lambda i, z: (0, 0)) for _ in range(4)],
            scratch_shapes=scratch,
        ),
        out_shape=[jax.ShapeDtypeStruct((K, width), F32) for _ in range(4)],
        compiler_params=PARAMS,
        name="left_product_first" if first else "left_product",
    )(z.reshape(1), *args, cross)


def right_product(left, squares, levels, cross, core):
    def kernel(core_ref, left_ref, squares_ref, levels_ref, cross_ref, own_ref, other_ref, shrunk_ref, both_ref, sum_ref, gram_ref):
        step = pl.program_id(0)

        @pl.when(step == 0)
        def _():
            values = shrunk_of(left_ref[...], squares_ref[...], levels_ref[...], 0, NV)
            shrunk_ref[...] = values
            gram_ref[...] = padded(cross_gram(values, values))
            both_ref[...] = jnp.concatenate(split2(values), axis=0)

        high, low = split2(cross_ref[...])
        both = both_ref[:, pl.ds(pl.multiple_of(step * BLOCK, BLOCK), BLOCK)]
        whole = dot(both, high, NN)
        product = whole[:K] + (whole[K:] + dot(both[:K], low, NN))

        @pl.when(step == 0)
        def _():
            sum_ref[...] = product

        @pl.when(step > 0)
        def _():
            sum_ref[...] += product

        @pl.when(step == ROWS // BLOCK - 1)
        def _():
            own = pl.multiple_of(core_ref[0] * HALF, HALF)
            other = pl.multiple_of((1 - core_ref[0]) * HALF, HALF)
            own_ref[:, :HALF] = sum_ref[:, pl.ds(own, HALF)]
            other_ref[:, :HALF] = sum_ref[:, pl.ds(other, HALF)]
            own_ref[:, HALF:] = gram_ref[...]
            other_ref[:, HALF:] = gram_ref[...]

    whole = lambda shape: pl.BlockSpec(shape, lambda i, c: (0, 0))
    return pl.pallas_call(
        kernel,
        grid_spec=pltpu.PrefetchScalarGridSpec(
            num_scalar_prefetch=1,
            grid=(ROWS // BLOCK,),
            in_specs=[
                whole((K, ROWS)),
                whole((1, LANES)),
                whole((2, K)),
                pl.BlockSpec((BLOCK, COLS), lambda i, c: (i, 0)),
            ],
            out_specs=[whole((K, HALF + LANES)), whole((K, HALF + LANES)), whole((K, ROWS))],
            scratch_shapes=[
                pltpu.VMEM((2 * K, ROWS), BF16),
                pltpu.VMEM((K, COLS), F32),
                pltpu.VMEM((K, LANES), F32),
            ],
        ),
        out_shape=[
            jax.ShapeDtypeStruct((K, HALF + LANES), F32),
            jax.ShapeDtypeStruct((K, HALF + LANES), F32),
            jax.ShapeDtypeStruct((K, ROWS), F32),
        ],
        compiler_params=PARAMS,
        name="right_product",
    )(core.reshape(1), left, squares, levels, cross)


def factor(gram, count):
    def kernel(gram_ref, out_ref):
        out_ref[...] = padded(inverse_factor(gram_ref[:, :K], count))

    return pl.pallas_call(
        kernel,
        out_shape=jax.ShapeDtypeStruct((K, LANES), F32),
        compiler_params=PARAMS,
        cost_estimate=pl.CostEstimate(flops=10_000_000, bytes_accessed=8_000_000, transcendentals=0),
        name="factor",
    )(gram)


def assemble(inverse, blocks, places, order):
    width = blocks[0].shape[1]
    n = len(blocks)

    def kernel(places_ref, *refs):
        if inverse is not None:
            inverse_ref, *refs = refs
        *ins, out_ref, squares_ref = refs
        total = jnp.zeros((K, 1), F32)
        for at, block in enumerate(ins):
            values = block[...]
            if inverse is not None:
                values = full_dot(inverse_ref[:, :K], values, NN)
            out_ref[:, pl.ds(pl.multiple_of(places_ref[at] * width, width), width)] = values
            total = total + jnp.sum(values * values, axis=1, keepdims=True)
        squares_ref[...] = to_row(total)

    args = blocks if inverse is None else [inverse, *blocks]
    vmem = pl.BlockSpec(memory_space=pltpu.VMEM)
    return pl.pallas_call(
        kernel,
        in_specs=[pl.BlockSpec(memory_space=pltpu.SMEM)] + [vmem] * len(args),
        out_specs=[vmem, vmem],
        out_shape=[
            jax.ShapeDtypeStruct((K, n * width), F32),
            jax.ShapeDtypeStruct((1, LANES), F32),
        ],
        compiler_params=PARAMS,
        name=order,
    )(places, *args)


def last_shrink(right_sum, squares, levels):
    def kernel(right_ref, squares_ref, levels_ref, shrunk_ref, out_ref):
        sums = right_ref[...]
        values = shrunk_of(sums, squares_ref[...], levels_ref[...], 1, NG)
        shrunk_ref[...] = values
        out_ref[...] = jnp.concatenate(
            [cross_gram(values, values), cross_gram(sums, values), jnp.zeros((K, LANES - 2 * K), F32)],
            axis=1,
        )

    return pl.pallas_call(
        kernel,
        out_shape=[
            jax.ShapeDtypeStruct((K, COLS), F32),
            jax.ShapeDtypeStruct((K, LANES), F32),
        ],
        compiler_params=PARAMS,
        name="last_shrink",
    )(right_sum, squares, levels)


def mix_left(inverse, shrunk):
    def kernel(inverse_ref, shrunk_ref, out_ref):
        out_ref[...] = full_dot(inverse_ref[:, :K], shrunk_ref[...], NN)

    return pl.pallas_call(
        kernel,
        out_shape=jax.ShapeDtypeStruct((K, ROWS), F32),
        compiler_params=PARAMS,
        name="mix_left",
    )(inverse, shrunk)


def deflate(last, right_shrunk, left_dirs, cross):
    def kernel(last_ref, shrunk_ref, left_ref, cross_ref, out_ref, right_ref, strength_ref, terms_ref, scale_ref):
        step = pl.program_id(0)

        @pl.when(step == 0)
        def _():
            inverse = inverse_factor(last_ref[:, :K], NG)
            right = full_dot(inverse, shrunk_ref[...], NN)
            right_ref[...] = right
            high, middle, low = split3(right)
            terms_ref[...] = jnp.concatenate([high, middle, high, low, middle, high], axis=0)
            strength = jnp.sum(inverse * last_ref[:, K : 2 * K], axis=1, keepdims=True) / math.sqrt(NV * NG)
            strength_ref[...] = to_row(strength)
            scale_ref[...] = jnp.broadcast_to(strength / math.sqrt(NV * NG), (K, LANES))

        scaled = left_ref[...] * scale_ref[:, :1]
        high, middle, low = split3(scaled)
        terms = jnp.concatenate([high, high, middle, high, middle, low], axis=0)
        out_ref[...] = cross_ref[...] - dot(terms, terms_ref[...], TN)

    whole = lambda shape: pl.BlockSpec(shape, lambda i: (0, 0))
    return pl.pallas_call(
        kernel,
        grid=(ROWS // BLOCK,),
        in_specs=[
            whole((K, LANES)),
            whole((K, COLS)),
            pl.BlockSpec((K, BLOCK), lambda i: (0, i)),
            pl.BlockSpec((BLOCK, COLS), lambda i: (i, 0)),
        ],
        out_specs=[
            pl.BlockSpec((BLOCK, COLS), lambda i: (i, 0)),
            whole((K, COLS)),
            whole((1, LANES)),
        ],
        out_shape=[
            jax.ShapeDtypeStruct((ROWS, COLS), F32),
            jax.ShapeDtypeStruct((K, COLS), F32),
            jax.ShapeDtypeStruct((1, LANES), F32),
        ],
        scratch_shapes=[pltpu.VMEM((6 * K, COLS), BF16), pltpu.VMEM((K, LANES), F32)],
        compiler_params=PARAMS,
        name="deflate",
    )(last, right_shrunk, left_dirs, cross)


def per_device(cross, start, levels):
    core = (lax.axis_index("vox") % 2).astype(jnp.int32)
    z = (lax.axis_index("var") % 4).astype(jnp.int32)
    quarters = jnp.stack([z] + [(z - step) % 4 for step in STEPS])
    halves = jnp.stack([core, 1 - core])
    right_sum, squares = start, None
    for sweep in range(ITERS):
        parts = left_product(right_sum, squares, levels, cross, z)
        total = parts[0]
        for step in STEPS:
            total = total + shift(parts[step], "var", Z_RINGS, step)
        total = ring_sum(total, "var", Y_RINGS)
        block = total[:, :QUARTER]
        blocks = [block] + [shift(block, "var", Z_RINGS, step) for step in STEPS]
        inverse = factor(total[:, QUARTER:], NG) if sweep else None
        left_sum, squares = assemble(inverse, blocks, quarters, "assemble_left")
        squares = ring_sum(pair_sum(squares), "vox", X_RINGS)

        own, other, left_shrunk = right_product(left_sum, squares, levels, cross, core)
        total = own + shift(other, "vox", CORE_PAIRS, 1)
        total = ring_sum(total, "vox", X_RINGS)
        block = total[:, :HALF]
        blocks = [block, shift(block, "vox", CORE_PAIRS, 1)]
        inverse = factor(total[:, HALF:], NV)
        right_sum, squares = assemble(inverse, blocks, halves, "assemble_right")
        squares = ring_sum(ring_sum(squares, "var", Y_RINGS), "var", Z_RINGS)
    left_dirs = mix_left(inverse, left_shrunk)
    right_shrunk, last = last_shrink(right_sum, squares, levels)
    last = ring_sum(ring_sum(last, "var", Y_RINGS), "var", Z_RINGS)
    deflated, right_dirs, strength = deflate(last, right_shrunk, left_dirs, cross)
    return (deflated, left_dirs, right_dirs, strength[0, :K])


def solution(mesh):
    in_specs = (P("vox", "var"), P(None, "var"), P())
    out_specs = (P("vox", "var"), P(None, "vox"), P(None, "var"), P())
    return jax.shard_map(
        per_device, mesh=mesh, in_specs=in_specs, out_specs=out_specs, check_vma=False
    )
```

```python
import math

import jax
import jax.numpy as jnp
from jax import lax
from jax.experimental import pallas as pl
from jax.experimental.pallas import tpu as pltpu
from jax.sharding import PartitionSpec as P

NV = 16384
NG = 24576
K = 32
ITERS = 2
ROWS = 2048
COLS = 1536
QUARTER = ROWS // 4
HALF = COLS // 2
BLOCK = 512
LANES = 128

EPSILON = 1e-06
HIGHEST = lax.Precision.HIGHEST
F32 = jnp.float32
BF16 = jnp.bfloat16
NT = (((1,), (1,)), ((), ()))
NN = (((1,), (0,)), ((), ()))
TN = (((0,), (0,)), ((), ()))

X_RINGS = [[x * 2 + c for x in range(4)] for c in range(2)]
CORE_PAIRS = [[x * 2, x * 2 + 1] for x in range(4)]
Y_RINGS = [[y * 4 + z for y in range(4)] for z in range(4)]
Z_RINGS = [[y * 4 + z for z in range(4)] for y in range(4)]
STEPS = (1, 3, 2)

PARAMS = pltpu.CompilerParams(vmem_limit_bytes=24 * 2**20)
FIRST_PARAMS = pltpu.CompilerParams(vmem_limit_bytes=40 * 2**20)


def shift(value, axis, rings, step):
    pairs = [(r[i], r[(i + step) % len(r)]) for r in rings for i in range(len(r))]
    return lax.ppermute(value, axis, pairs)


def ring_sum(value, axis, rings):
    got = [shift(value, axis, rings, step) for step in STEPS]
    return (value + got[0]) + (got[1] + got[2])


def pair_sum(value):
    return value + shift(value, "vox", CORE_PAIRS, 1)


def dot(a, b, dims):
    return lax.dot_general(a, b, dims, preferred_element_type=F32)


def full_dot(a, b, dims):
    return lax.dot_general(a, b, dims, precision=HIGHEST, preferred_element_type=F32)


def split2(x):
    high = x.astype(BF16)
    return high, (x - high.astype(F32)).astype(BF16)


def split3(x):
    high = x.astype(BF16)
    rest = x - high.astype(F32)
    middle = rest.astype(BF16)
    return high, middle, (rest - middle.astype(F32)).astype(BF16)


def diagonal(width=LANES, offset=0):
    row = lax.broadcasted_iota(jnp.int32, (K, width), 0)
    lane = lax.broadcasted_iota(jnp.int32, (K, width), 1)
    return lane == row + offset


def to_column(row):
    return jnp.sum(jnp.where(diagonal(K), row, 0.0), axis=1, keepdims=True)


def to_row(column):
    return jnp.sum(jnp.where(diagonal(), column, 0.0), axis=0, keepdims=True)


def cross_gram(a, b):
    parts = dot(jnp.concatenate(split3(a), axis=0), jnp.concatenate(split3(b), axis=0), NT)
    rows = parts[:K] + (parts[K : 2 * K] + parts[2 * K :])
    return rows[:, :K] + (rows[:, K : 2 * K] + rows[:, 2 * K :])


def shrunk_of(values, squares, levels, side, count):
    thresholds = levels[side : side + 1, :].astype(F32) / 1024.0
    level = to_column(thresholds * jnp.sqrt(squares[:, :K] / count + EPSILON))
    return values - jnp.clip(values, -level, level)


def padded(small):
    return jnp.concatenate([small, jnp.zeros((K, LANES - small.shape[1]), F32)], axis=1)


def inverse_factor(gram, count):
    start = gram / count + jnp.where(diagonal(K), EPSILON, 0.0)
    start = jnp.concatenate(
        [jnp.where(diagonal(K), 1.0, 0.0), start, jnp.zeros((K, LANES - 2 * K), F32)], axis=1
    )
    blocks = [start[8 * b : 8 * b + 8] for b in range(4)]
    row = lax.broadcasted_iota(jnp.int32, (8, LANES), 0)
    pivots = []
    for panel in range(4):
        columns = [
            {
                b: jnp.broadcast_to(blocks[b][:, K + 8 * panel + t : K + 8 * panel + t + 1], (8, LANES))
                for b in range(panel, 4)
            }
            for t in range(8)
        ]
        pivot_of = jnp.ones((8, LANES), F32)
        for t in range(8):
            pivot = columns[t][panel][t : t + 1]
            pivot_of = jnp.where(row == t, pivot, pivot_of)
            inverse = 1.0 / pivot
            top = blocks[panel][t : t + 1]
            for b in range(panel, 4):
                factor = columns[t][b] * inverse
                if b == panel:
                    factor = jnp.where(row > t, factor, 0.0)
                columns[t][b] = factor
            for u in range(t + 1, 8):
                head = columns[u][panel][t : t + 1]
                for b in range(panel, 4):
                    columns[u][b] = columns[u][b] - columns[t][b] * head
            for b in range(panel, 4):
                blocks[b] = blocks[b] - columns[t][b] * top
        pivots.append(pivot_of)
    scale = 1.0 / jnp.sqrt(jnp.concatenate(pivots, axis=0))
    return (jnp.concatenate(blocks, axis=0) * scale)[:, :K]


Z_AT, CORE_AT = 0, 4


def own_places():
    def kernel(out_ref):
        z = lax.rem(lax.axis_index("var"), 4)
        core = lax.rem(lax.axis_index("vox"), 2)
        out_ref[Z_AT] = z
        for at, step in enumerate(STEPS):
            out_ref[Z_AT + 1 + at] = lax.rem(z + 4 - step, 4)
        out_ref[CORE_AT] = core
        out_ref[CORE_AT + 1] = 1 - core
        out_ref[6] = 0
        out_ref[7] = 0

    return pl.pallas_call(
        kernel,
        out_specs=pl.BlockSpec(memory_space=pltpu.SMEM),
        out_shape=jax.ShapeDtypeStruct((8,), jnp.int32),
        compiler_params=PARAMS,
        name="own_places",
    )()


def left_product(right, squares, levels, cross, places):
    first = squares is None
    width = QUARTER if first else QUARTER + LANES

    def kernel(z_ref, *refs):
        if first:
            right_ref, cross_ref, *outs, kept_ref, both_ref = refs
        else:
            right_ref, squares_ref, levels_ref, cross_ref, *outs, both_ref, gram_ref = refs
        step = pl.program_id(0)

        @pl.when(step == 0)
        def _():
            values = right_ref[...]
            if not first:
                values = shrunk_of(values, squares_ref[...], levels_ref[...], 1, NG)
                gram_ref[...] = padded(cross_gram(values, values))
            both_ref[...] = jnp.concatenate(split2(values), axis=0)

        block = cross_ref[...]
        if first:
            kept_ref[...] = block
        high, low = split2(block)
        whole = dot(both_ref[...], high, NT)
        product = whole[:K] + (whole[K:] + dot(both_ref[:K], low, NT))
        for at in range(4):

            @pl.when(step == at)
            def _():
                outs[at][:, :QUARTER] = product
                if not first:
                    outs[at][:, QUARTER:] = gram_ref[...]

    small = [] if first else [
        pl.BlockSpec((1, LANES), lambda i, z: (0, 0)),
        pl.BlockSpec((2, K), lambda i, z: (0, 0)),
    ]
    scratch = [pltpu.VMEM((2 * K, COLS), BF16)]
    if not first:
        scratch.append(pltpu.VMEM((K, LANES), F32))
    args = (right,) if first else (right, squares, levels)
    return pl.pallas_call(
        kernel,
        grid_spec=pltpu.PrefetchScalarGridSpec(
            num_scalar_prefetch=1,
            grid=(4,),
            in_specs=[pl.BlockSpec((K, COLS), lambda i, z: (0, 0))]
            + small
            + [pl.BlockSpec((QUARTER, COLS), lambda i, z: (lax.rem(z[Z_AT] + i, 4), 0))],
            out_specs=[pl.BlockSpec((K, width), lambda i, z: (0, 0)) for _ in range(4)]
            + [pl.BlockSpec((QUARTER, COLS), lambda i, z: (lax.rem(z[Z_AT] + i, 4), 0))] * first,
            scratch_shapes=scratch,
        ),
        out_shape=[jax.ShapeDtypeStruct((K, width), F32) for _ in range(4)]
        + [jax.ShapeDtypeStruct((ROWS, COLS), F32)] * first,
        compiler_params=FIRST_PARAMS if first else PARAMS,
        name="left_product_first" if first else "left_product",
    )(places, *args, cross)


def right_product(left, squares, levels, cross, places):
    def kernel(core_ref, left_ref, squares_ref, levels_ref, cross_ref, own_ref, other_ref, shrunk_ref, both_ref, sum_ref, gram_ref):
        step = pl.program_id(0)

        @pl.when(step == 0)
        def _():
            values = shrunk_of(left_ref[...], squares_ref[...], levels_ref[...], 0, NV)
            shrunk_ref[...] = values
            gram_ref[...] = padded(cross_gram(values, values))
            both_ref[...] = jnp.concatenate(split2(values), axis=0)

        high, low = split2(cross_ref[...])
        both = both_ref[:, pl.ds(pl.multiple_of(step * BLOCK, BLOCK), BLOCK)]
        whole = dot(both, high, NN)
        product = whole[:K] + (whole[K:] + dot(both[:K], low, NN))

        @pl.when(step == 0)
        def _():
            sum_ref[...] = product

        @pl.when(step > 0)
        def _():
            sum_ref[...] += product

        @pl.when(step == ROWS // BLOCK - 1)
        def _():
            own = pl.multiple_of(core_ref[CORE_AT] * HALF, HALF)
            other = pl.multiple_of((1 - core_ref[CORE_AT]) * HALF, HALF)
            own_ref[:, :HALF] = sum_ref[:, pl.ds(own, HALF)]
            other_ref[:, :HALF] = sum_ref[:, pl.ds(other, HALF)]
            own_ref[:, HALF:] = gram_ref[...]
            other_ref[:, HALF:] = gram_ref[...]

    whole = lambda shape: pl.BlockSpec(shape, lambda i, c: (0, 0))
    return pl.pallas_call(
        kernel,
        grid_spec=pltpu.PrefetchScalarGridSpec(
            num_scalar_prefetch=1,
            grid=(ROWS // BLOCK,),
            in_specs=[
                whole((K, ROWS)),
                whole((1, LANES)),
                whole((2, K)),
                pl.BlockSpec((BLOCK, COLS), lambda i, c: (i, 0)),
            ],
            out_specs=[whole((K, HALF + LANES)), whole((K, HALF + LANES)), whole((K, ROWS))],
            scratch_shapes=[
                pltpu.VMEM((2 * K, ROWS), BF16),
                pltpu.VMEM((K, COLS), F32),
                pltpu.VMEM((K, LANES), F32),
            ],
        ),
        out_shape=[
            jax.ShapeDtypeStruct((K, HALF + LANES), F32),
            jax.ShapeDtypeStruct((K, HALF + LANES), F32),
            jax.ShapeDtypeStruct((K, ROWS), F32),
        ],
        compiler_params=PARAMS,
        name="right_product",
    )(places, left, squares, levels, cross)


def factor(gram, count):
    def kernel(gram_ref, out_ref):
        out_ref[...] = padded(inverse_factor(gram_ref[:, :K], count))

    return pl.pallas_call(
        kernel,
        out_shape=jax.ShapeDtypeStruct((K, LANES), F32),
        compiler_params=PARAMS,
        cost_estimate=pl.CostEstimate(flops=10_000_000, bytes_accessed=8_000_000, transcendentals=0),
        name="factor",
    )(gram)


def assemble(inverse, blocks, places, start, order):
    width = blocks[0].shape[1]
    n = len(blocks)

    def kernel(places_ref, *refs):
        if inverse is not None:
            inverse_ref, *refs = refs
        *ins, out_ref, squares_ref = refs
        total = jnp.zeros((K, 1), F32)
        for at, block in enumerate(ins):
            values = block[...]
            if inverse is not None:
                values = full_dot(inverse_ref[:, :K], values, NN)
            out_ref[:, pl.ds(pl.multiple_of(places_ref[start + at] * width, width), width)] = values
            total = total + jnp.sum(values * values, axis=1, keepdims=True)
        squares_ref[...] = to_row(total)

    args = blocks if inverse is None else [inverse, *blocks]
    vmem = pl.BlockSpec(memory_space=pltpu.VMEM)
    return pl.pallas_call(
        kernel,
        in_specs=[pl.BlockSpec(memory_space=pltpu.SMEM)] + [vmem] * len(args),
        out_specs=[vmem, vmem],
        out_shape=[
            jax.ShapeDtypeStruct((K, n * width), F32),
            jax.ShapeDtypeStruct((1, LANES), F32),
        ],
        compiler_params=PARAMS,
        name=order,
    )(places, *args)


def last_shrink(right_sum, squares, levels):
    def kernel(right_ref, squares_ref, levels_ref, shrunk_ref, out_ref):
        sums = right_ref[...]
        values = shrunk_of(sums, squares_ref[...], levels_ref[...], 1, NG)
        shrunk_ref[...] = values
        out_ref[...] = jnp.concatenate(
            [cross_gram(values, values), cross_gram(sums, values), jnp.zeros((K, LANES - 2 * K), F32)],
            axis=1,
        )

    return pl.pallas_call(
        kernel,
        out_shape=[
            jax.ShapeDtypeStruct((K, COLS), F32),
            jax.ShapeDtypeStruct((K, LANES), F32),
        ],
        compiler_params=PARAMS,
        name="last_shrink",
    )(right_sum, squares, levels)


def mix_left(inverse, shrunk):
    def kernel(inverse_ref, shrunk_ref, out_ref, terms_ref):
        left = full_dot(inverse_ref[:, :K], shrunk_ref[...], NN)
        out_ref[...] = left
        high, middle, low = split3(left)
        terms_ref[...] = jnp.concatenate([high, high, middle, high, middle, low], axis=0)

    return pl.pallas_call(
        kernel,
        out_shape=[
            jax.ShapeDtypeStruct((K, ROWS), F32),
            jax.ShapeDtypeStruct((6 * K, ROWS), BF16),
        ],
        compiler_params=PARAMS,
        name="mix_left",
    )(inverse, shrunk)


def deflate(last, right_shrunk, left_terms, cross):
    def kernel(last_ref, shrunk_ref, left_ref, cross_ref, out_ref, right_ref, strength_ref, terms_ref):
        step = pl.program_id(0)

        @pl.when(step == 0)
        def _():
            inverse = inverse_factor(last_ref[:, :K], NG)
            right = full_dot(inverse, shrunk_ref[...], NN)
            right_ref[...] = right
            strength = jnp.sum(inverse * last_ref[:, K : 2 * K], axis=1, keepdims=True) / math.sqrt(NV * NG)
            strength_ref[...] = to_row(strength)[:, :K]
            high, middle, low = split3(right * (strength / math.sqrt(NV * NG)))
            terms_ref[...] = jnp.concatenate([high, middle, high, low, middle, high], axis=0)

        out_ref[...] = cross_ref[...] - dot(left_ref[...], terms_ref[...], TN)

    whole = lambda shape: pl.BlockSpec(shape, lambda i: (0, 0))
    return pl.pallas_call(
        kernel,
        grid=(ROWS // BLOCK,),
        in_specs=[
            whole((K, LANES)),
            whole((K, COLS)),
            pl.BlockSpec((6 * K, BLOCK), lambda i: (0, i)),
            pl.BlockSpec((BLOCK, COLS), lambda i: (i, 0)),
        ],
        out_specs=[
            pl.BlockSpec((BLOCK, COLS), lambda i: (i, 0)),
            whole((K, COLS)),
            whole((1, K)),
        ],
        out_shape=[
            jax.ShapeDtypeStruct((ROWS, COLS), F32),
            jax.ShapeDtypeStruct((K, COLS), F32),
            jax.ShapeDtypeStruct((1, K), F32),
        ],
        scratch_shapes=[pltpu.VMEM((6 * K, COLS), BF16)],
        compiler_params=PARAMS,
        name="deflate",
    )(last, right_shrunk, left_terms, cross)


def per_device(cross, start, levels):
    places = own_places()
    right_sum, squares = start, None
    for sweep in range(ITERS):
        parts = left_product(right_sum, squares, levels, cross, places)
        if sweep == 0:
            cross = parts[4]
        total = parts[0]
        for step in STEPS:
            total = total + shift(parts[step], "var", Z_RINGS, step)
        total = ring_sum(total, "var", Y_RINGS)
        block = total[:, :QUARTER]
        blocks = [block] + [shift(block, "var", Z_RINGS, step) for step in STEPS]
        inverse = factor(total[:, QUARTER:], NG) if sweep else None
        left_sum, squares = assemble(inverse, blocks, places, Z_AT, "assemble_left")
        squares = ring_sum(pair_sum(squares), "vox", X_RINGS)

        own, other, left_shrunk = right_product(left_sum, squares, levels, cross, places)
        total = own + shift(other, "vox", CORE_PAIRS, 1)
        total = ring_sum(total, "vox", X_RINGS)
        block = total[:, :HALF]
        blocks = [block, shift(block, "vox", CORE_PAIRS, 1)]
        inverse = factor(total[:, HALF:], NV)
        right_sum, squares = assemble(inverse, blocks, places, CORE_AT, "assemble_right")
        squares = ring_sum(ring_sum(squares, "var", Y_RINGS), "var", Z_RINGS)
    left_dirs, left_terms = mix_left(inverse, left_shrunk)
    right_shrunk, last = last_shrink(right_sum, squares, levels)
    last = ring_sum(ring_sum(last, "var", Y_RINGS), "var", Z_RINGS)
    deflated, right_dirs, strength = deflate(last, right_shrunk, left_terms, cross)
    return (deflated, left_dirs, right_dirs, strength.reshape(K))


def solution(mesh):
    in_specs = (P("vox", "var"), P(None, "var"), P())
    out_specs = (P("vox", "var"), P(None, "vox"), P(None, "var"), P())
    return jax.shard_map(
        per_device, mesh=mesh, in_specs=in_specs, out_specs=out_specs, check_vma=False
    )
```

```python
import math

import jax
import jax.numpy as jnp
from jax import lax
from jax.experimental import pallas as pl
from jax.experimental.pallas import tpu as pltpu
from jax.sharding import PartitionSpec as P

NV = 16384
NG = 24576
K = 32
ITERS = 2
ROWS = 2048
COLS = 1536
QUARTER = ROWS // 4
HALF = COLS // 2
BLOCK = 512
LANES = 128

EPSILON = 1e-06
HIGHEST = lax.Precision.HIGHEST
F32 = jnp.float32
BF16 = jnp.bfloat16
NT = (((1,), (1,)), ((), ()))
NN = (((1,), (0,)), ((), ()))
TN = (((0,), (0,)), ((), ()))

X_RINGS = [[x * 2 + c for x in range(4)] for c in range(2)]
CORE_PAIRS = [[x * 2, x * 2 + 1] for x in range(4)]
Y_RINGS = [[y * 4 + z for y in range(4)] for z in range(4)]
Z_RINGS = [[y * 4 + z for z in range(4)] for y in range(4)]
MASKS = (1, 3, 2)

PARAMS = pltpu.CompilerParams(vmem_limit_bytes=24 * 2**20)
FIRST_PARAMS = pltpu.CompilerParams(vmem_limit_bytes=40 * 2**20)


def swap(value, axis, rings, mask):
    pairs = [(r[i], r[i ^ mask]) for r in rings for i in range(len(r))]
    return lax.ppermute(value, axis, pairs)


def ring_sum(value, axis, rings):
    got = [swap(value, axis, rings, mask) for mask in MASKS]
    return (value + got[0]) + (got[1] + got[2])


def pair_sum(value):
    return value + swap(value, "vox", CORE_PAIRS, 1)


def dot(a, b, dims):
    return lax.dot_general(a, b, dims, preferred_element_type=F32)


def full_dot(a, b, dims):
    return lax.dot_general(a, b, dims, precision=HIGHEST, preferred_element_type=F32)


def split2(x):
    high = x.astype(BF16)
    return high, (x - high.astype(F32)).astype(BF16)


def split3(x):
    high = x.astype(BF16)
    rest = x - high.astype(F32)
    middle = rest.astype(BF16)
    return high, middle, (rest - middle.astype(F32)).astype(BF16)


def diagonal(width=LANES, offset=0):
    row = lax.broadcasted_iota(jnp.int32, (K, width), 0)
    lane = lax.broadcasted_iota(jnp.int32, (K, width), 1)
    return lane == row + offset


def to_column(row):
    return jnp.sum(jnp.where(diagonal(K), row, 0.0), axis=1, keepdims=True)


def to_row(column):
    return jnp.sum(jnp.where(diagonal(), column, 0.0), axis=0, keepdims=True)


def cross_gram(a, b):
    parts = dot(jnp.concatenate(split3(a), axis=0), jnp.concatenate(split3(b), axis=0), NT)
    rows = parts[:K] + (parts[K : 2 * K] + parts[2 * K :])
    return rows[:, :K] + (rows[:, K : 2 * K] + rows[:, 2 * K :])


def shrunk_of(values, squares, levels, side, count):
    thresholds = levels[side : side + 1, :].astype(F32) / 1024.0
    level = to_column(thresholds * jnp.sqrt(squares[:, :K] / count + EPSILON))
    return values - jnp.clip(values, -level, level)


def padded(small):
    return jnp.concatenate([small, jnp.zeros((K, LANES - small.shape[1]), F32)], axis=1)


def inverse_factor(gram, count):
    start = gram / count + jnp.where(diagonal(K), EPSILON, 0.0)
    start = jnp.concatenate(
        [jnp.where(diagonal(K), 1.0, 0.0), start, jnp.zeros((K, LANES - 2 * K), F32)], axis=1
    )
    blocks = [start[8 * b : 8 * b + 8] for b in range(4)]
    row = lax.broadcasted_iota(jnp.int32, (8, LANES), 0)
    pivots = []
    for panel in range(4):
        columns = [
            {
                b: jnp.broadcast_to(blocks[b][:, K + 8 * panel + t : K + 8 * panel + t + 1], (8, LANES))
                for b in range(panel, 4)
            }
            for t in range(8)
        ]
        pivot_of = jnp.ones((8, LANES), F32)
        for t in range(8):
            pivot = columns[t][panel][t : t + 1]
            pivot_of = jnp.where(row == t, pivot, pivot_of)
            inverse = 1.0 / pivot
            top = blocks[panel][t : t + 1]
            for b in range(panel, 4):
                factor = columns[t][b] * inverse
                if b == panel:
                    factor = jnp.where(row > t, factor, 0.0)
                columns[t][b] = factor
            for u in range(t + 1, 8):
                head = columns[u][panel][t : t + 1]
                for b in range(panel, 4):
                    columns[u][b] = columns[u][b] - columns[t][b] * head
            for b in range(panel, 4):
                blocks[b] = blocks[b] - columns[t][b] * top
        pivots.append(pivot_of)
    scale = 1.0 / jnp.sqrt(jnp.concatenate(pivots, axis=0))
    return (jnp.concatenate(blocks, axis=0) * scale)[:, :K]


Z_AT, CORE_AT = 0, 4


def own_places():
    def kernel(out_ref):
        z = lax.rem(lax.axis_index("var"), 4)
        core = lax.rem(lax.axis_index("vox"), 2)
        out_ref[Z_AT] = z
        for at, mask in enumerate(MASKS):
            out_ref[Z_AT + 1 + at] = lax.bitwise_xor(z, jnp.int32(mask))
        out_ref[CORE_AT] = core
        out_ref[CORE_AT + 1] = 1 - core
        out_ref[6] = 0
        out_ref[7] = 0

    return pl.pallas_call(
        kernel,
        out_specs=pl.BlockSpec(memory_space=pltpu.SMEM),
        out_shape=jax.ShapeDtypeStruct((8,), jnp.int32),
        compiler_params=PARAMS,
        name="own_places",
    )()


def left_product_first(right, cross, places):
    def kernel(places_ref, right_ref, cross_ref, *refs):
        *outs, kept_ref, both_ref = refs
        step = pl.program_id(0)

        @pl.when(step == 0)
        def _():
            both_ref[...] = jnp.concatenate(split2(right_ref[...]), axis=0)

        block = cross_ref[...]
        kept_ref[...] = block
        product = left_terms_of(both_ref, block)
        for at in range(4):

            @pl.when(step == at)
            def _():
                outs[at][...] = product

    quarter = pl.BlockSpec((QUARTER, COLS), lambda i, p: (p[Z_AT + i], 0))
    return pl.pallas_call(
        kernel,
        grid_spec=pltpu.PrefetchScalarGridSpec(
            num_scalar_prefetch=1,
            grid=(4,),
            in_specs=[pl.BlockSpec((K, COLS), lambda i, p: (0, 0)), quarter],
            out_specs=[pl.BlockSpec((K, QUARTER), lambda i, p: (0, 0))] * 4 + [quarter],
            scratch_shapes=[pltpu.VMEM((2 * K, COLS), BF16)],
        ),
        out_shape=[jax.ShapeDtypeStruct((K, QUARTER), F32)] * 4
        + [jax.ShapeDtypeStruct((ROWS, COLS), F32)],
        compiler_params=FIRST_PARAMS,
        name="left_product_first",
    )(places, right, cross)


def left_terms_of(both_ref, block):
    high, low = split2(block)
    whole = dot(both_ref[...], high, NT)
    return whole[:K] + (whole[K:] + dot(both_ref[:K], low, NT))


def left_partners(right_sum, squares, levels, cross, places):
    def kernel(places_ref, right_ref, squares_ref, levels_ref, cross_ref, *refs):
        *outs, both_ref, gram_ref = refs
        step = pl.program_id(0)

        @pl.when(step == 0)
        def _():
            values = shrunk_of(right_ref[...], squares_ref[...], levels_ref[...], 1, NG)
            both_ref[...] = jnp.concatenate(split2(values), axis=0)
            gram_ref[...] = padded(cross_gram(values, values))

        product = left_terms_of(both_ref, cross_ref[...])
        for at in range(3):

            @pl.when(step == at)
            def _():
                outs[at][:, :QUARTER] = product
                outs[at][:, QUARTER:] = gram_ref[...]

    whole = lambda shape: pl.BlockSpec(shape, lambda i, p: (0, 0))
    shapes = [((K, QUARTER + LANES), F32)] * 3 + [((2 * K, COLS), BF16), ((K, LANES), F32)]
    return pl.pallas_call(
        kernel,
        grid_spec=pltpu.PrefetchScalarGridSpec(
            num_scalar_prefetch=1,
            grid=(3,),
            in_specs=[whole((K, COLS)), whole((1, LANES)), whole((2, K))]
            + [pl.BlockSpec((QUARTER, COLS), lambda i, p: (p[Z_AT + 1 + i], 0))],
            out_specs=[whole(shape) for shape, _ in shapes],
        ),
        out_shape=[jax.ShapeDtypeStruct(*shape) for shape in shapes],
        compiler_params=PARAMS,
        name="left_partners",
    )(places, right_sum, squares, levels, cross)


def left_own(both, gram, cross, places):
    def kernel(places_ref, both_ref, gram_ref, cross_ref, out_ref):
        out_ref[:, :QUARTER] = left_terms_of(both_ref, cross_ref[...])
        out_ref[:, QUARTER:] = gram_ref[...]

    whole = lambda shape: pl.BlockSpec(shape, lambda i, p: (0, 0))
    return pl.pallas_call(
        kernel,
        grid_spec=pltpu.PrefetchScalarGridSpec(
            num_scalar_prefetch=1,
            grid=(1,),
            in_specs=[whole((2 * K, COLS)), whole((K, LANES))]
            + [pl.BlockSpec((QUARTER, COLS), lambda i, p: (p[Z_AT], 0))],
            out_specs=whole((K, QUARTER + LANES)),
        ),
        out_shape=jax.ShapeDtypeStruct((K, QUARTER + LANES), F32),
        compiler_params=PARAMS,
        cost_estimate=pl.CostEstimate(flops=600_000_000, bytes_accessed=4_000_000, transcendentals=0),
        name="left_own",
    )(places, both, gram, cross)


def right_half(head, given, cross, places, at):
    def kernel(places_ref, *refs):
        step = pl.program_id(0)
        if head:
            left_ref, squares_ref, levels_ref, cross_ref, out_ref, both_ref, gram_ref, shrunk_ref = refs

            @pl.when(step == 0)
            def _():
                values = shrunk_of(left_ref[...], squares_ref[...], levels_ref[...], 0, NV)
                shrunk_ref[...] = values
                both_ref[...] = jnp.concatenate(split2(values), axis=0)
                gram_ref[...] = padded(cross_gram(values, values))
        else:
            both_ref, gram_ref, cross_ref, out_ref = refs
        high, low = split2(cross_ref[...])
        both = both_ref[:, pl.ds(pl.multiple_of(step * BLOCK, BLOCK), BLOCK)]
        whole = dot(both, high, NN)
        product = whole[:K] + (whole[K:] + dot(both[:K], low, NN))

        @pl.when(step == 0)
        def _():
            out_ref[:, :HALF] = product
            out_ref[:, HALF:] = gram_ref[...]

        @pl.when(step > 0)
        def _():
            out_ref[:, :HALF] += product

    whole = lambda shape: pl.BlockSpec(shape, lambda i, p: (0, 0))
    out_shape = [jax.ShapeDtypeStruct((K, HALF + LANES), F32)]
    if head:
        out_shape += [
            jax.ShapeDtypeStruct((2 * K, ROWS), BF16),
            jax.ShapeDtypeStruct((K, LANES), F32),
            jax.ShapeDtypeStruct((K, ROWS), F32),
        ]
    return pl.pallas_call(
        kernel,
        grid_spec=pltpu.PrefetchScalarGridSpec(
            num_scalar_prefetch=1,
            grid=(ROWS // BLOCK,),
            in_specs=[whole(g.shape) for g in given]
            + [pl.BlockSpec((BLOCK, HALF), lambda i, p: (i, p[CORE_AT + at]))],
            out_specs=[whole(o.shape) for o in out_shape],
        ),
        out_shape=out_shape,
        compiler_params=PARAMS,
        cost_estimate=pl.CostEstimate(flops=1_200_000_000, bytes_accessed=8_000_000, transcendentals=0),
        name="right_half_head" if head else "right_half",
    )(places, *given, cross)


def factor(gram, count):
    def kernel(gram_ref, out_ref):
        out_ref[...] = padded(inverse_factor(gram_ref[:, :K], count))

    return pl.pallas_call(
        kernel,
        out_shape=jax.ShapeDtypeStruct((K, LANES), F32),
        compiler_params=PARAMS,
        cost_estimate=pl.CostEstimate(flops=10_000_000, bytes_accessed=8_000_000, transcendentals=0),
        name="factor",
    )(gram)


def assemble(inverse, blocks, places, start, order):
    width = blocks[0].shape[1]
    n = len(blocks)

    def kernel(places_ref, *refs):
        if inverse is not None:
            inverse_ref, *refs = refs
        *ins, out_ref, squares_ref = refs
        total = jnp.zeros((K, 1), F32)
        for at, block in enumerate(ins):
            values = block[...]
            if inverse is not None:
                values = full_dot(inverse_ref[:, :K], values, NN)
            out_ref[:, pl.ds(pl.multiple_of(places_ref[start + at] * width, width), width)] = values
            total = total + jnp.sum(values * values, axis=1, keepdims=True)
        squares_ref[...] = to_row(total)

    args = blocks if inverse is None else [inverse, *blocks]
    vmem = pl.BlockSpec(memory_space=pltpu.VMEM)
    return pl.pallas_call(
        kernel,
        in_specs=[pl.BlockSpec(memory_space=pltpu.SMEM)] + [vmem] * len(args),
        out_specs=[vmem, vmem],
        out_shape=[
            jax.ShapeDtypeStruct((K, n * width), F32),
            jax.ShapeDtypeStruct((1, LANES), F32),
        ],
        compiler_params=PARAMS,
        name=order,
    )(places, *args)


def last_shrink(right_sum, squares, levels):
    def kernel(right_ref, squares_ref, levels_ref, shrunk_ref, out_ref):
        sums = right_ref[...]
        values = shrunk_of(sums, squares_ref[...], levels_ref[...], 1, NG)
        shrunk_ref[...] = values
        out_ref[...] = jnp.concatenate(
            [cross_gram(values, values), cross_gram(sums, values), jnp.zeros((K, LANES - 2 * K), F32)],
            axis=1,
        )

    return pl.pallas_call(
        kernel,
        out_shape=[
            jax.ShapeDtypeStruct((K, COLS), F32),
            jax.ShapeDtypeStruct((K, LANES), F32),
        ],
        compiler_params=PARAMS,
        name="last_shrink",
    )(right_sum, squares, levels)


def mix_left(inverse, shrunk):
    def kernel(inverse_ref, shrunk_ref, out_ref, terms_ref):
        left = full_dot(inverse_ref[:, :K], shrunk_ref[...], NN)
        out_ref[...] = left
        high, middle, low = split3(left)
        terms_ref[...] = jnp.concatenate([high, high, middle, high, middle, low], axis=0)

    return pl.pallas_call(
        kernel,
        out_shape=[
            jax.ShapeDtypeStruct((K, ROWS), F32),
            jax.ShapeDtypeStruct((6 * K, ROWS), BF16),
        ],
        compiler_params=PARAMS,
        name="mix_left",
    )(inverse, shrunk)


def deflate(last, right_shrunk, left_terms, cross):
    def kernel(last_ref, shrunk_ref, left_ref, cross_ref, out_ref, right_ref, strength_ref, terms_ref):
        step = pl.program_id(0)

        @pl.when(step == 0)
        def _():
            inverse = inverse_factor(last_ref[:, :K], NG)
            right = full_dot(inverse, shrunk_ref[...], NN)
            right_ref[...] = right
            strength = jnp.sum(inverse * last_ref[:, K : 2 * K], axis=1, keepdims=True) / math.sqrt(NV * NG)
            strength_ref[...] = to_row(strength)[:, :K]
            high, middle, low = split3(right * (strength / math.sqrt(NV * NG)))
            terms_ref[...] = jnp.concatenate([high, middle, high, low, middle, high], axis=0)

        out_ref[...] = cross_ref[...] - dot(left_ref[...], terms_ref[...], TN)

    whole = lambda shape: pl.BlockSpec(shape, lambda i: (0, 0))
    return pl.pallas_call(
        kernel,
        grid=(ROWS // BLOCK,),
        in_specs=[
            whole((K, LANES)),
            whole((K, COLS)),
            pl.BlockSpec((6 * K, BLOCK), lambda i: (0, i)),
            pl.BlockSpec((BLOCK, COLS), lambda i: (i, 0)),
        ],
        out_specs=[
            pl.BlockSpec((BLOCK, COLS), lambda i: (i, 0)),
            whole((K, COLS)),
            whole((1, K)),
        ],
        out_shape=[
            jax.ShapeDtypeStruct((ROWS, COLS), F32),
            jax.ShapeDtypeStruct((K, COLS), F32),
            jax.ShapeDtypeStruct((1, K), F32),
        ],
        scratch_shapes=[pltpu.VMEM((6 * K, COLS), BF16)],
        compiler_params=PARAMS,
        name="deflate",
    )(last, right_shrunk, left_terms, cross)


def per_device(cross, start, levels):
    places = own_places()
    for sweep in range(ITERS):
        if sweep == 0:
            *parts, cross = left_product_first(start, cross, places)
            got = [swap(parts[at + 1], "var", Z_RINGS, mask) for at, mask in enumerate(MASKS)]
            total = parts[0]
        else:
            *parts, both, gram = left_partners(right_sum, squares, levels, cross, places)
            got = [swap(part, "var", Z_RINGS, mask) for part, mask in zip(parts, MASKS)]
            total = left_own(both, gram, cross, places)
        total = (total + got[0]) + (got[1] + got[2])
        total = ring_sum(total, "var", Y_RINGS)
        block = total[:, :QUARTER]
        blocks = [block] + [swap(block, "var", Z_RINGS, mask) for mask in MASKS]
        inverse = factor(total[:, QUARTER:], NG) if sweep else None
        left_sum, squares = assemble(inverse, blocks, places, Z_AT, "assemble_left")
        squares = ring_sum(pair_sum(squares), "vox", X_RINGS)

        part, both, gram, left_shrunk = right_half(True, (left_sum, squares, levels), cross, places, 1)
        got = swap(part, "vox", CORE_PAIRS, 1)
        (total,) = right_half(False, (both, gram), cross, places, 0)
        total = ring_sum(total + got, "vox", X_RINGS)
        block = total[:, :HALF]
        blocks = [block, swap(block, "vox", CORE_PAIRS, 1)]
        inverse = factor(total[:, HALF:], NV)
        right_sum, squares = assemble(inverse, blocks, places, CORE_AT, "assemble_right")
        squares = ring_sum(ring_sum(squares, "var", Y_RINGS), "var", Z_RINGS)
    left_dirs, left_terms = mix_left(inverse, left_shrunk)
    right_shrunk, last = last_shrink(right_sum, squares, levels)
    last = ring_sum(ring_sum(last, "var", Y_RINGS), "var", Z_RINGS)
    deflated, right_dirs, strength = deflate(last, right_shrunk, left_terms, cross)
    return (deflated, left_dirs, right_dirs, strength.reshape(K))


def solution(mesh):
    in_specs = (P("vox", "var"), P(None, "var"), P())
    out_specs = (P("vox", "var"), P(None, "vox"), P(None, "var"), P())
    return jax.shard_map(
        per_device, mesh=mesh, in_specs=in_specs, out_specs=out_specs, check_vma=False
    )
```

```python
import math

import jax
import jax.numpy as jnp
from jax import lax
from jax.experimental import pallas as pl
from jax.experimental.pallas import tpu as pltpu
from jax.sharding import PartitionSpec as P

NV = 16384
NG = 24576
K = 32
ITERS = 2
ROWS = 2048
COLS = 1536
QUARTER = ROWS // 4
HALF = COLS // 2
BLOCK = 1024
LANES = 128

EPSILON = 1e-06
HIGHEST = lax.Precision.HIGHEST
F32 = jnp.float32
BF16 = jnp.bfloat16
NT = (((1,), (1,)), ((), ()))
NN = (((1,), (0,)), ((), ()))

X_RINGS = [[x * 2 + c for x in range(4)] for c in range(2)]
CORE_PAIRS = [[x * 2, x * 2 + 1] for x in range(4)]
Y_RINGS = [[y * 4 + z for y in range(4)] for z in range(4)]
Z_RINGS = [[y * 4 + z for z in range(4)] for y in range(4)]
MASKS = (1, 3, 2)

PARAMS = pltpu.CompilerParams(vmem_limit_bytes=24 * 2**20)
FIRST_PARAMS = pltpu.CompilerParams(vmem_limit_bytes=40 * 2**20)


def swap(value, axis, rings, mask):
    pairs = [(r[i], r[i ^ mask]) for r in rings for i in range(len(r))]
    return lax.ppermute(value, axis, pairs)


def ring_sum(value, axis, rings):
    got = [swap(value, axis, rings, mask) for mask in MASKS]
    return (value + got[0]) + (got[1] + got[2])


def from_all(value):
    return lax.all_to_all(value, "var", 0, 0)


def pair_sum(value):
    return value + swap(value, "vox", CORE_PAIRS, 1)


def dot(a, b, dims):
    return lax.dot_general(a, b, dims, preferred_element_type=F32)


def full_dot(a, b, dims):
    return lax.dot_general(a, b, dims, precision=HIGHEST, preferred_element_type=F32)


def split2(x):
    high = x.astype(BF16)
    return high, (x - high.astype(F32)).astype(BF16)


def split3(x):
    high = x.astype(BF16)
    rest = x - high.astype(F32)
    middle = rest.astype(BF16)
    return high, middle, (rest - middle.astype(F32)).astype(BF16)


def diagonal(width=LANES, offset=0):
    row = lax.broadcasted_iota(jnp.int32, (K, width), 0)
    lane = lax.broadcasted_iota(jnp.int32, (K, width), 1)
    return lane == row + offset


def to_column(row):
    return jnp.sum(jnp.where(diagonal(K), row, 0.0), axis=1, keepdims=True)


def to_row(column):
    return jnp.sum(jnp.where(diagonal(), column, 0.0), axis=0, keepdims=True)


def cross_gram(a, b):
    parts = dot(jnp.concatenate(split3(a), axis=0), jnp.concatenate(split3(b), axis=0), NT)
    rows = parts[:K] + (parts[K : 2 * K] + parts[2 * K :])
    return rows[:, :K] + (rows[:, K : 2 * K] + rows[:, 2 * K :])


def shrunk_of(values, squares, levels, side, count):
    squares = jnp.sum(squares, axis=0)
    thresholds = levels[side : side + 1, :].astype(F32) / 1024.0
    level = to_column(thresholds * jnp.sqrt(squares[:, :K] / count + EPSILON))
    return values - jnp.clip(values, -level, level)


def padded(small):
    return jnp.concatenate([small, jnp.zeros((K, LANES - small.shape[1]), F32)], axis=1)


def inverse_factor(gram, count):
    start = gram / count + jnp.where(diagonal(K), EPSILON, 0.0)
    start = jnp.concatenate(
        [jnp.where(diagonal(K), 1.0, 0.0), start, jnp.zeros((K, LANES - 2 * K), F32)], axis=1
    )
    blocks = [start[8 * b : 8 * b + 8] for b in range(4)]
    row = lax.broadcasted_iota(jnp.int32, (8, LANES), 0)
    pivots = []
    for panel in range(4):
        columns = [
            {
                b: jnp.broadcast_to(blocks[b][:, K + 8 * panel + t : K + 8 * panel + t + 1], (8, LANES))
                for b in range(panel, 4)
            }
            for t in range(8)
        ]
        pivot_of = jnp.ones((8, LANES), F32)
        for t in range(8):
            pivot = columns[t][panel][t : t + 1]
            pivot_of = jnp.where(row == t, pivot, pivot_of)
            inverse = 1.0 / pivot
            top = blocks[panel][t : t + 1]
            for b in range(panel, 4):
                factor = columns[t][b] * inverse
                if b == panel:
                    factor = jnp.where(row > t, factor, 0.0)
                columns[t][b] = factor
            for u in range(t + 1, 8):
                head = columns[u][panel][t : t + 1]
                for b in range(panel, 4):
                    columns[u][b] = columns[u][b] - columns[t][b] * head
            for b in range(panel, 4):
                blocks[b] = blocks[b] - columns[t][b] * top
        pivots.append(pivot_of)
    scale = 1.0 / jnp.sqrt(jnp.concatenate(pivots, axis=0))
    return (jnp.concatenate(blocks, axis=0) * scale)[:, :K]


Z_AT, CORE_AT = 0, 4


def own_places():
    def kernel(out_ref):
        z = lax.rem(lax.axis_index("var"), 4)
        core = lax.rem(lax.axis_index("vox"), 2)
        out_ref[Z_AT] = z
        for at, mask in enumerate(MASKS):
            out_ref[Z_AT + 1 + at] = lax.bitwise_xor(z, jnp.int32(mask))
        out_ref[CORE_AT] = core
        out_ref[CORE_AT + 1] = 1 - core
        out_ref[6] = 0
        out_ref[7] = 0

    return pl.pallas_call(
        kernel,
        out_specs=pl.BlockSpec(memory_space=pltpu.SMEM),
        out_shape=jax.ShapeDtypeStruct((8,), jnp.int32),
        compiler_params=PARAMS,
        name="own_places",
    )()


def left_product_first(right, cross, places):
    def kernel(places_ref, right_ref, cross_ref, *refs):
        *outs, kept_ref, both_ref = refs
        step = pl.program_id(0)

        @pl.when(step == 0)
        def _():
            both_ref[...] = jnp.concatenate(split2(right_ref[...]), axis=0)

        block = cross_ref[...]
        kept_ref[...] = block
        product = left_terms_of(both_ref, block)
        for at in range(4):

            @pl.when(step == at)
            def _():
                outs[at][...] = product

    quarter = pl.BlockSpec((QUARTER, COLS), lambda i, p: (p[Z_AT + i], 0))
    return pl.pallas_call(
        kernel,
        grid_spec=pltpu.PrefetchScalarGridSpec(
            num_scalar_prefetch=1,
            grid=(4,),
            in_specs=[pl.BlockSpec((K, COLS), lambda i, p: (0, 0)), quarter],
            out_specs=[pl.BlockSpec((K, QUARTER), lambda i, p: (0, 0))] * 4 + [quarter],
            scratch_shapes=[pltpu.VMEM((2 * K, COLS), BF16)],
        ),
        out_shape=[jax.ShapeDtypeStruct((K, QUARTER), F32)] * 4
        + [jax.ShapeDtypeStruct((ROWS, COLS), F32)],
        compiler_params=FIRST_PARAMS,
        name="left_product_first",
    )(places, right, cross)


def left_terms_of(both_ref, block):
    high, low = split2(block)
    whole = dot(both_ref[...], high, NT)
    return whole[:K] + (whole[K:] + dot(both_ref[:K], low, NT))


def left_partners(right_sum, squares, levels, cross, places):
    def kernel(places_ref, right_ref, squares_ref, levels_ref, cross_ref, *refs):
        *outs, both_ref, gram_ref = refs
        step = pl.program_id(0)

        @pl.when(step == 0)
        def _():
            values = shrunk_of(right_ref[...], squares_ref[...], levels_ref[...], 1, NG)
            both_ref[...] = jnp.concatenate(split2(values), axis=0)
            gram_ref[...] = padded(cross_gram(values, values))

        product = left_terms_of(both_ref, cross_ref[...])
        for at in range(3):

            @pl.when(step == at)
            def _():
                outs[at][:, :QUARTER] = product
                outs[at][:, QUARTER:] = gram_ref[...]

    whole = lambda shape: pl.BlockSpec(shape, lambda i, p: (0,) * len(shape))
    shapes = [((K, QUARTER + LANES), F32)] * 3 + [((2 * K, COLS), BF16), ((K, LANES), F32)]
    return pl.pallas_call(
        kernel,
        grid_spec=pltpu.PrefetchScalarGridSpec(
            num_scalar_prefetch=1,
            grid=(3,),
            in_specs=[whole((K, COLS)), whole((16, 1, LANES)), whole((2, K))]
            + [pl.BlockSpec((QUARTER, COLS), lambda i, p: (p[Z_AT + 1 + i], 0))],
            out_specs=[whole(shape) for shape, _ in shapes],
        ),
        out_shape=[jax.ShapeDtypeStruct(*shape) for shape in shapes],
        compiler_params=PARAMS,
        name="left_partners",
    )(places, right_sum, squares, levels, cross)


def left_own(both, gram, cross, places):
    def kernel(places_ref, both_ref, gram_ref, cross_ref, out_ref):
        out_ref[:, :QUARTER] = left_terms_of(both_ref, cross_ref[...])
        out_ref[:, QUARTER:] = gram_ref[...]

    whole = lambda shape: pl.BlockSpec(shape, lambda i, p: (0,) * len(shape))
    return pl.pallas_call(
        kernel,
        grid_spec=pltpu.PrefetchScalarGridSpec(
            num_scalar_prefetch=1,
            grid=(1,),
            in_specs=[whole((2 * K, COLS)), whole((K, LANES))]
            + [pl.BlockSpec((QUARTER, COLS), lambda i, p: (p[Z_AT], 0))],
            out_specs=whole((K, QUARTER + LANES)),
        ),
        out_shape=jax.ShapeDtypeStruct((K, QUARTER + LANES), F32),
        compiler_params=PARAMS,
        cost_estimate=pl.CostEstimate(flops=600_000_000, bytes_accessed=4_000_000, transcendentals=0),
        name="left_own",
    )(places, both, gram, cross)


def right_half(head, given, cross, places, at):
    def kernel(places_ref, *refs):
        if head:
            left_ref, squares_ref, levels_ref, cross_ref, out_ref, both_ref, gram_ref, shrunk_ref = refs

            values = shrunk_of(left_ref[...], squares_ref[...], levels_ref[...], 0, NV)
            shrunk_ref[...] = values
            both_ref[...] = jnp.concatenate(split2(values), axis=0)
            gram_ref[...] = padded(cross_gram(values, values))
        else:
            both_ref, gram_ref, cross_ref, out_ref = refs
        high, low = split2(cross_ref[...])
        product = dot(both_ref[...], high, NN)
        out_ref[:, :HALF] = product[:K] + (product[K:] + dot(both_ref[:K], low, NN))
        out_ref[:, HALF:] = gram_ref[...]

    whole = lambda shape: pl.BlockSpec(shape, lambda i, p: (0,) * len(shape))
    out_shape = [jax.ShapeDtypeStruct((K, HALF + LANES), F32)]
    if head:
        out_shape += [
            jax.ShapeDtypeStruct((2 * K, ROWS), BF16),
            jax.ShapeDtypeStruct((K, LANES), F32),
            jax.ShapeDtypeStruct((K, ROWS), F32),
        ]
    return pl.pallas_call(
        kernel,
        grid_spec=pltpu.PrefetchScalarGridSpec(
            num_scalar_prefetch=1,
            grid=(1,),
            in_specs=[whole(g.shape) for g in given]
            + [pl.BlockSpec((ROWS, HALF), lambda i, p: (0, p[CORE_AT + at]))],
            out_specs=[whole(o.shape) for o in out_shape],
        ),
        out_shape=out_shape,
        compiler_params=PARAMS,
        cost_estimate=pl.CostEstimate(flops=1_200_000_000, bytes_accessed=8_000_000, transcendentals=0),
        name="right_half_head" if head else "right_half",
    )(places, *given, cross)


def factor(gram, count):
    def kernel(gram_ref, out_ref):
        out_ref[...] = padded(inverse_factor(gram_ref[:, :K], count))

    return pl.pallas_call(
        kernel,
        out_shape=jax.ShapeDtypeStruct((K, LANES), F32),
        compiler_params=PARAMS,
        cost_estimate=pl.CostEstimate(flops=10_000_000, bytes_accessed=8_000_000, transcendentals=0),
        name="factor",
    )(gram)


def assemble(inverse, blocks, places, start, copies, order):
    width = blocks[0].shape[1]
    n = len(blocks)

    def kernel(places_ref, *refs):
        if inverse is not None:
            inverse_ref, *refs = refs
        *ins, out_ref, squares_ref = refs
        total = jnp.zeros((K, 1), F32)
        for at, block in enumerate(ins):
            values = block[...]
            if inverse is not None:
                values = full_dot(inverse_ref[:, :K], values, NN)
            out_ref[:, pl.ds(pl.multiple_of(places_ref[start + at] * width, width), width)] = values
            total = total + jnp.sum(values * values, axis=1, keepdims=True)
        squares_ref[...] = jnp.broadcast_to(to_row(total)[None], (copies, 1, LANES))

    args = blocks if inverse is None else [inverse, *blocks]
    vmem = pl.BlockSpec(memory_space=pltpu.VMEM)
    return pl.pallas_call(
        kernel,
        in_specs=[pl.BlockSpec(memory_space=pltpu.SMEM)] + [vmem] * len(args),
        out_specs=[vmem, vmem],
        out_shape=[
            jax.ShapeDtypeStruct((K, n * width), F32),
            jax.ShapeDtypeStruct((copies, 1, LANES), F32),
        ],
        compiler_params=PARAMS,
        name=order,
    )(places, *args)


def last_shrink(right_sum, squares, levels):
    def kernel(right_ref, squares_ref, levels_ref, shrunk_ref, out_ref):
        sums = right_ref[...]
        values = shrunk_of(sums, squares_ref[...], levels_ref[...], 1, NG)
        shrunk_ref[...] = values
        both = jnp.concatenate([cross_gram(values, values), cross_gram(sums, values)], axis=1)
        packed = jnp.concatenate([both[: K // 2], both[K // 2 :]], axis=1)
        out_ref[...] = jnp.broadcast_to(packed[None], (16, K // 2, LANES))

    return pl.pallas_call(
        kernel,
        out_shape=[
            jax.ShapeDtypeStruct((K, COLS), F32),
            jax.ShapeDtypeStruct((16, K // 2, LANES), F32),
        ],
        compiler_params=PARAMS,
        name="last_shrink",
    )(right_sum, squares, levels)


def mix_left(inverse, shrunk):
    def kernel(inverse_ref, shrunk_ref, out_ref, terms_ref):
        left = full_dot(inverse_ref[:, :K], shrunk_ref[...], NN)
        out_ref[...] = left
        high, middle, low = split3(left)
        terms_ref[...] = jnp.concatenate([high, high, middle, high, middle, low], axis=0).T

    return pl.pallas_call(
        kernel,
        out_shape=[
            jax.ShapeDtypeStruct((K, ROWS), F32),
            jax.ShapeDtypeStruct((ROWS, 6 * K), BF16),
        ],
        compiler_params=PARAMS,
        name="mix_left",
    )(inverse, shrunk)


def deflate(last, right_shrunk, left_terms, cross):
    def kernel(last_ref, shrunk_ref, left_ref, cross_ref, out_ref, right_ref, strength_ref, terms_ref):
        step = pl.program_id(0)

        @pl.when(step == 0)
        def _():
            packed = jnp.sum(last_ref[...], axis=0)
            last = jnp.concatenate([packed[:, : 2 * K], packed[:, 2 * K :]], axis=0)
            inverse = inverse_factor(last[:, :K], NG)
            right = full_dot(inverse, shrunk_ref[...], NN)
            right_ref[...] = right
            strength = jnp.sum(inverse * last[:, K:], axis=1, keepdims=True) / math.sqrt(NV * NG)
            strength_ref[...] = to_row(strength)[:, :K]
            high, middle, low = split3(right * (strength / math.sqrt(NV * NG)))
            terms_ref[...] = jnp.concatenate([high, middle, high, low, middle, high], axis=0)

        out_ref[...] = cross_ref[...] - dot(left_ref[...], terms_ref[...], NN)

    whole = lambda shape: pl.BlockSpec(shape, lambda i: (0,) * len(shape))
    return pl.pallas_call(
        kernel,
        grid=(ROWS // BLOCK,),
        in_specs=[
            whole((16, K // 2, LANES)),
            whole((K, COLS)),
            pl.BlockSpec((BLOCK, 6 * K), lambda i: (i, 0)),
            pl.BlockSpec((BLOCK, COLS), lambda i: (i, 0)),
        ],
        out_specs=[
            pl.BlockSpec((BLOCK, COLS), lambda i: (i, 0)),
            whole((K, COLS)),
            whole((1, K)),
        ],
        out_shape=[
            jax.ShapeDtypeStruct((ROWS, COLS), F32),
            jax.ShapeDtypeStruct((K, COLS), F32),
            jax.ShapeDtypeStruct((1, K), F32),
        ],
        scratch_shapes=[pltpu.VMEM((6 * K, COLS), BF16)],
        compiler_params=PARAMS,
        name="deflate",
    )(last, right_shrunk, left_terms, cross)


def per_device(cross, start, levels):
    places = own_places()
    for sweep in range(ITERS):
        if sweep == 0:
            *parts, cross = left_product_first(start, cross, places)
            got = [swap(parts[at + 1], "var", Z_RINGS, mask) for at, mask in enumerate(MASKS)]
            total = parts[0]
        else:
            *parts, both, gram = left_partners(right_sum, squares, levels, cross, places)
            got = [swap(part, "var", Z_RINGS, mask) for part, mask in zip(parts, MASKS)]
            total = left_own(both, gram, cross, places)
        total = (total + got[0]) + (got[1] + got[2])
        total = ring_sum(total, "var", Y_RINGS)
        block = total[:, :QUARTER]
        blocks = [block] + [swap(block, "var", Z_RINGS, mask) for mask in MASKS]
        inverse = factor(total[:, QUARTER:], NG) if sweep else None
        left_sum, squares = assemble(inverse, blocks, places, Z_AT, 1, "assemble_left")
        squares = ring_sum(pair_sum(squares), "vox", X_RINGS)

        part, both, gram, left_shrunk = right_half(True, (left_sum, squares, levels), cross, places, 1)
        got = swap(part, "vox", CORE_PAIRS, 1)
        (total,) = right_half(False, (both, gram), cross, places, 0)
        total = ring_sum(total + got, "vox", X_RINGS)
        block = total[:, :HALF]
        got = swap(block, "vox", CORE_PAIRS, 1)
        inverse = factor(total[:, HALF:], NV)
        if sweep == ITERS - 1:
            left_dirs, left_terms = mix_left(inverse, left_shrunk)
            got, left_terms = lax.optimization_barrier((got, left_terms))
        blocks = [block, got]
        right_sum, squares = assemble(inverse, blocks, places, CORE_AT, 16, "assemble_right")
        squares = from_all(squares)
    right_shrunk, last = last_shrink(right_sum, squares, levels)
    last = from_all(last)
    deflated, right_dirs, strength = deflate(last, right_shrunk, left_terms, cross)
    return (deflated, left_dirs, right_dirs, strength.reshape(K))


def solution(mesh):
    in_specs = (P("vox", "var"), P(None, "var"), P())
    out_specs = (P("vox", "var"), P(None, "vox"), P(None, "var"), P())
    return jax.shard_map(
        per_device, mesh=mesh, in_specs=in_specs, out_specs=out_specs, check_vma=False
    )
```

```python
import math

import jax
import jax.numpy as jnp
from jax import lax
from jax.experimental import pallas as pl
from jax.experimental.pallas import tpu as pltpu
from jax.sharding import PartitionSpec as P

NV = 16384
NG = 24576
K = 32
ITERS = 2
ROWS = 2048
COLS = 1536
QUARTER = ROWS // 4
HALF = COLS // 2
BLOCK = 1024
LANES = 128

EPSILON = 1e-06
F32 = jnp.float32
BF16 = jnp.bfloat16
NT = (((1,), (1,)), ((), ()))
NN = (((1,), (0,)), ((), ()))

X_RINGS = [[x * 2 + c for x in range(4)] for c in range(2)]
CORE_PAIRS = [[x * 2, x * 2 + 1] for x in range(4)]
Y_RINGS = [[y * 4 + z for y in range(4)] for z in range(4)]
Z_RINGS = [[y * 4 + z for z in range(4)] for y in range(4)]
MASKS = (1, 3, 2)

PARAMS = pltpu.CompilerParams(vmem_limit_bytes=24 * 2**20)
FIRST_PARAMS = pltpu.CompilerParams(vmem_limit_bytes=40 * 2**20)


def swap(value, axis, rings, mask):
    pairs = [(r[i], r[i ^ mask]) for r in rings for i in range(len(r))]
    return lax.ppermute(value, axis, pairs)


def ring_sum(value, axis, rings):
    got = [swap(value, axis, rings, mask) for mask in MASKS]
    return (value + got[0]) + (got[1] + got[2])


def from_all(value):
    return lax.all_to_all(value, "var", 0, 0)


def pair_sum(value):
    return value + swap(value, "vox", CORE_PAIRS, 1)


def dot(a, b, dims):
    return lax.dot_general(a, b, dims, preferred_element_type=F32)


def split2(x):
    high = x.astype(BF16)
    return high, (x - high.astype(F32)).astype(BF16)


def split3(x):
    high = x.astype(BF16)
    rest = x - high.astype(F32)
    middle = rest.astype(BF16)
    return high, middle, (rest - middle.astype(F32)).astype(BF16)


def mixed(matrix, values):
    high, middle, low = split3(matrix)
    left = jnp.concatenate([low, middle, high, middle, high, high], axis=1)
    high, middle, low = split3(values)
    return dot(left, jnp.concatenate([high, middle, low, high, middle, high], axis=0), NN)


def diagonal(width=LANES, offset=0):
    row = lax.broadcasted_iota(jnp.int32, (K, width), 0)
    lane = lax.broadcasted_iota(jnp.int32, (K, width), 1)
    return lane == row + offset


def to_column(row):
    return jnp.sum(jnp.where(diagonal(K), row, 0.0), axis=1, keepdims=True)


def to_row(column):
    return jnp.sum(jnp.where(diagonal(), column, 0.0), axis=0, keepdims=True)


def cross_gram(a, b):
    parts = dot(jnp.concatenate(split3(a), axis=0), jnp.concatenate(split3(b), axis=0), NT)
    rows = parts[:K] + (parts[K : 2 * K] + parts[2 * K :])
    return rows[:, :K] + (rows[:, K : 2 * K] + rows[:, 2 * K :])


def shrunk_of(values, squares, levels, side, count):
    squares = jnp.sum(squares, axis=0)
    thresholds = levels[side : side + 1, :].astype(F32) / 1024.0
    level = to_column(thresholds * jnp.sqrt(squares[:, :K] / count + EPSILON))
    return values - jnp.clip(values, -level, level)


def padded(small):
    return jnp.concatenate([small, jnp.zeros((K, LANES - small.shape[1]), F32)], axis=1)


def inverse_factor(gram, count):
    start = gram / count + jnp.where(diagonal(K), EPSILON, 0.0)
    start = jnp.concatenate(
        [jnp.where(diagonal(K), 1.0, 0.0), start, jnp.zeros((K, LANES - 2 * K), F32)], axis=1
    )
    blocks = [start[8 * b : 8 * b + 8] for b in range(4)]
    row = lax.broadcasted_iota(jnp.int32, (8, LANES), 0)
    pivots = []
    for panel in range(4):
        columns = [
            {
                b: jnp.broadcast_to(blocks[b][:, K + 8 * panel + t : K + 8 * panel + t + 1], (8, LANES))
                for b in range(panel, 4)
            }
            for t in range(8)
        ]
        pivot_of = jnp.ones((8, LANES), F32)
        for t in range(8):
            pivot = columns[t][panel][t : t + 1]
            pivot_of = jnp.where(row == t, pivot, pivot_of)
            inverse = 1.0 / pivot
            top = blocks[panel][t : t + 1]
            for b in range(panel, 4):
                factor = columns[t][b] * inverse
                if b == panel:
                    factor = jnp.where(row > t, factor, 0.0)
                columns[t][b] = factor
            for u in range(t + 1, 8):
                head = columns[u][panel][t : t + 1]
                for b in range(panel, 4):
                    columns[u][b] = columns[u][b] - columns[t][b] * head
            for b in range(panel, 4):
                blocks[b] = blocks[b] - columns[t][b] * top
        pivots.append(pivot_of)
    scale = 1.0 / jnp.sqrt(jnp.concatenate(pivots, axis=0))
    return (jnp.concatenate(blocks, axis=0) * scale)[:, :K]


Z_AT, CORE_AT = 0, 4


def left_product_first(right, cross):
    chunk = QUARTER // 2
    chunks = ROWS // chunk
    ahead = 3

    def kernel(right_hbm, cross_hbm, *refs):
        *outs, kept_ref, places_ref, right_ref, right_sem, sems = refs
        z = lax.rem(lax.axis_index("var"), 4)
        core = lax.rem(lax.axis_index("vox"), 2)
        places = [z] + [lax.bitwise_xor(z, jnp.int32(mask)) for mask in MASKS]

        def rows_of(at):
            first = places[at // 2] * QUARTER + (at % 2) * chunk
            return pl.ds(pl.multiple_of(first, chunk), chunk)

        def copy_of(at):
            return pltpu.make_async_copy(
                cross_hbm.at[rows_of(at), :], kept_ref.at[rows_of(at), :], sems.at[at]
            )

        right_copy = pltpu.make_async_copy(right_hbm, right_ref, right_sem)
        right_copy.start()
        for at in range(ahead):
            copy_of(at).start()
        for at, place in enumerate(places):
            places_ref[Z_AT + at] = place
        places_ref[CORE_AT] = core
        places_ref[CORE_AT + 1] = 1 - core
        places_ref[6] = 0
        places_ref[7] = 0
        right_copy.wait()
        both = jnp.concatenate(split2(right_ref[...]), axis=0)
        for quarter in range(4):
            for at in (2 * quarter, 2 * quarter + 1):
                copy_of(at).wait()
                if at + ahead < chunks:
                    copy_of(at + ahead).start()
            rows = pl.ds(pl.multiple_of(places[quarter] * QUARTER, QUARTER), QUARTER)
            outs[quarter][...] = left_terms_of(both, kept_ref[rows, :])

    vmem = pl.BlockSpec(memory_space=pltpu.VMEM)
    hbm = pl.BlockSpec(memory_space=pltpu.HBM)
    return pl.pallas_call(
        kernel,
        in_specs=[hbm, hbm],
        out_specs=[vmem] * 5 + [pl.BlockSpec(memory_space=pltpu.SMEM)],
        out_shape=[jax.ShapeDtypeStruct((K, QUARTER), F32)] * 4
        + [jax.ShapeDtypeStruct((ROWS, COLS), F32), jax.ShapeDtypeStruct((8,), jnp.int32)],
        scratch_shapes=[
            pltpu.VMEM((K, COLS), F32),
            pltpu.SemaphoreType.DMA,
            pltpu.SemaphoreType.DMA((chunks,)),
        ],
        compiler_params=FIRST_PARAMS,
        name="left_product_first",
    )(right, cross)


def left_terms_of(both, block):
    high, low = split2(block)
    whole = dot(both, high, NT)
    return whole[:K] + (whole[K:] + dot(both[:K], low, NT))


def left_partners(right_sum, squares, levels, cross, places):
    def kernel(places_ref, right_ref, squares_ref, levels_ref, cross_ref, *refs):
        *outs, both_ref, gram_ref = refs
        step = pl.program_id(0)

        @pl.when(step == 0)
        def _():
            values = shrunk_of(right_ref[...], squares_ref[...], levels_ref[...], 1, NG)
            both_ref[...] = jnp.concatenate(split2(values), axis=0)
            gram_ref[...] = padded(cross_gram(values, values))

        product = left_terms_of(both_ref[...], cross_ref[...])
        for at in range(3):

            @pl.when(step == at)
            def _():
                outs[at][:, :QUARTER] = product
                outs[at][:, QUARTER:] = gram_ref[...]

    whole = lambda shape: pl.BlockSpec(shape, lambda i, p: (0,) * len(shape))
    shapes = [((K, QUARTER + LANES), F32)] * 3 + [((2 * K, COLS), BF16), ((K, LANES), F32)]
    return pl.pallas_call(
        kernel,
        grid_spec=pltpu.PrefetchScalarGridSpec(
            num_scalar_prefetch=1,
            grid=(3,),
            in_specs=[whole((K, COLS)), whole((16, 1, LANES)), whole((2, K))]
            + [pl.BlockSpec((QUARTER, COLS), lambda i, p: (p[Z_AT + 1 + i], 0))],
            out_specs=[whole(shape) for shape, _ in shapes],
        ),
        out_shape=[jax.ShapeDtypeStruct(*shape) for shape in shapes],
        compiler_params=PARAMS,
        name="left_partners",
    )(places, right_sum, squares, levels, cross)


def left_own(both, gram, cross, places):
    def kernel(places_ref, both_ref, gram_ref, cross_ref, out_ref):
        out_ref[:, :QUARTER] = left_terms_of(both_ref[...], cross_ref[...])
        out_ref[:, QUARTER:] = gram_ref[...]

    whole = lambda shape: pl.BlockSpec(shape, lambda i, p: (0,) * len(shape))
    return pl.pallas_call(
        kernel,
        grid_spec=pltpu.PrefetchScalarGridSpec(
            num_scalar_prefetch=1,
            grid=(1,),
            in_specs=[whole((2 * K, COLS)), whole((K, LANES))]
            + [pl.BlockSpec((QUARTER, COLS), lambda i, p: (p[Z_AT], 0))],
            out_specs=whole((K, QUARTER + LANES)),
        ),
        out_shape=jax.ShapeDtypeStruct((K, QUARTER + LANES), F32),
        compiler_params=PARAMS,
        cost_estimate=pl.CostEstimate(flops=600_000_000, bytes_accessed=4_000_000, transcendentals=0),
        name="left_own",
    )(places, both, gram, cross)


def right_half(head, given, cross, places, at):
    def kernel(places_ref, *refs):
        if head:
            left_ref, squares_ref, levels_ref, cross_ref, out_ref, both_ref, gram_ref, shrunk_ref = refs

            values = shrunk_of(left_ref[...], squares_ref[...], levels_ref[...], 0, NV)
            shrunk_ref[...] = values
            both_ref[...] = jnp.concatenate(split2(values), axis=0)
            gram_ref[...] = padded(cross_gram(values, values))
        else:
            both_ref, gram_ref, cross_ref, out_ref = refs
        high, low = split2(cross_ref[...])
        product = dot(both_ref[...], high, NN)
        out_ref[:, :HALF] = product[:K] + (product[K:] + dot(both_ref[:K], low, NN))
        out_ref[:, HALF:] = gram_ref[...]

    whole = lambda shape: pl.BlockSpec(shape, lambda i, p: (0,) * len(shape))
    out_shape = [jax.ShapeDtypeStruct((K, HALF + LANES), F32)]
    if head:
        out_shape += [
            jax.ShapeDtypeStruct((2 * K, ROWS), BF16),
            jax.ShapeDtypeStruct((K, LANES), F32),
            jax.ShapeDtypeStruct((K, ROWS), F32),
        ]
    return pl.pallas_call(
        kernel,
        grid_spec=pltpu.PrefetchScalarGridSpec(
            num_scalar_prefetch=1,
            grid=(1,),
            in_specs=[whole(g.shape) for g in given]
            + [pl.BlockSpec((ROWS, HALF), lambda i, p: (0, p[CORE_AT + at]))],
            out_specs=[whole(o.shape) for o in out_shape],
        ),
        out_shape=out_shape,
        compiler_params=PARAMS,
        cost_estimate=pl.CostEstimate(flops=1_200_000_000, bytes_accessed=8_000_000, transcendentals=0),
        name="right_half_head" if head else "right_half",
    )(places, *given, cross)


def factor(gram, count):
    def kernel(gram_ref, out_ref):
        out_ref[...] = padded(inverse_factor(gram_ref[:, :K], count))

    return pl.pallas_call(
        kernel,
        out_shape=jax.ShapeDtypeStruct((K, LANES), F32),
        compiler_params=PARAMS,
        cost_estimate=pl.CostEstimate(flops=10_000_000, bytes_accessed=8_000_000, transcendentals=0),
        name="factor",
    )(gram)


def assemble(inverse, blocks, places, start, copies, order):
    width = blocks[0].shape[1]
    n = len(blocks)

    def kernel(places_ref, *refs):
        if inverse is not None:
            inverse_ref, *refs = refs
        *ins, out_ref, squares_ref = refs
        total = jnp.zeros((K, 1), F32)
        for at, block in enumerate(ins):
            values = block[...]
            if inverse is not None:
                values = mixed(inverse_ref[:, :K], values)
            out_ref[:, pl.ds(pl.multiple_of(places_ref[start + at] * width, width), width)] = values
            total = total + jnp.sum(values * values, axis=1, keepdims=True)
        squares_ref[...] = jnp.broadcast_to(to_row(total)[None], (copies, 1, LANES))

    args = blocks if inverse is None else [inverse, *blocks]
    vmem = pl.BlockSpec(memory_space=pltpu.VMEM)
    return pl.pallas_call(
        kernel,
        in_specs=[pl.BlockSpec(memory_space=pltpu.SMEM)] + [vmem] * len(args),
        out_specs=[vmem, vmem],
        out_shape=[
            jax.ShapeDtypeStruct((K, n * width), F32),
            jax.ShapeDtypeStruct((copies, 1, LANES), F32),
        ],
        compiler_params=PARAMS,
        name=order,
    )(places, *args)


def last_shrink(right_sum, squares, levels):
    def kernel(right_ref, squares_ref, levels_ref, shrunk_ref, out_ref):
        sums = right_ref[...]
        values = shrunk_of(sums, squares_ref[...], levels_ref[...], 1, NG)
        shrunk_ref[...] = values
        both = jnp.concatenate([cross_gram(values, values), cross_gram(sums, values)], axis=1)
        packed = jnp.concatenate([both[: K // 2], both[K // 2 :]], axis=1)
        out_ref[...] = jnp.broadcast_to(packed[None], (16, K // 2, LANES))

    return pl.pallas_call(
        kernel,
        out_shape=[
            jax.ShapeDtypeStruct((K, COLS), F32),
            jax.ShapeDtypeStruct((16, K // 2, LANES), F32),
        ],
        compiler_params=PARAMS,
        name="last_shrink",
    )(right_sum, squares, levels)


def mix_left(inverse, shrunk):
    def kernel(inverse_ref, shrunk_ref, out_ref, terms_ref):
        left = mixed(inverse_ref[:, :K], shrunk_ref[...])
        out_ref[...] = left
        high, middle, low = split3(left)
        terms_ref[...] = jnp.concatenate([high, high, middle, high, middle, low], axis=0).T

    return pl.pallas_call(
        kernel,
        out_shape=[
            jax.ShapeDtypeStruct((K, ROWS), F32),
            jax.ShapeDtypeStruct((ROWS, 6 * K), BF16),
        ],
        compiler_params=PARAMS,
        name="mix_left",
    )(inverse, shrunk)


def deflate(last, right_shrunk, left_terms, cross):
    def kernel(last_ref, shrunk_ref, left_ref, cross_ref, out_ref, right_ref, strength_ref, terms_ref):
        step = pl.program_id(0)

        @pl.when(step == 0)
        def _():
            packed = jnp.sum(last_ref[...], axis=0)
            last = jnp.concatenate([packed[:, : 2 * K], packed[:, 2 * K :]], axis=0)
            inverse = inverse_factor(last[:, :K], NG)
            right = mixed(inverse, shrunk_ref[...])
            right_ref[...] = right
            strength = jnp.sum(inverse * last[:, K:], axis=1, keepdims=True) / math.sqrt(NV * NG)
            strength_ref[...] = to_row(strength)[:, :K]
            high, middle, low = split3(right * (strength / math.sqrt(NV * NG)))
            terms_ref[...] = jnp.concatenate([high, middle, high, low, middle, high], axis=0)

        out_ref[...] = cross_ref[...] - dot(left_ref[...], terms_ref[...], NN)

    whole = lambda shape: pl.BlockSpec(shape, lambda i: (0,) * len(shape))
    return pl.pallas_call(
        kernel,
        grid=(ROWS // BLOCK,),
        in_specs=[
            whole((16, K // 2, LANES)),
            whole((K, COLS)),
            pl.BlockSpec((BLOCK, 6 * K), lambda i: (i, 0)),
            pl.BlockSpec((BLOCK, COLS), lambda i: (i, 0)),
        ],
        out_specs=[
            pl.BlockSpec((BLOCK, COLS), lambda i: (i, 0)),
            whole((K, COLS)),
            whole((1, K)),
        ],
        out_shape=[
            jax.ShapeDtypeStruct((ROWS, COLS), F32),
            jax.ShapeDtypeStruct((K, COLS), F32),
            jax.ShapeDtypeStruct((1, K), F32),
        ],
        scratch_shapes=[pltpu.VMEM((6 * K, COLS), BF16)],
        compiler_params=PARAMS,
        name="deflate",
    )(last, right_shrunk, left_terms, cross)


def per_device(cross, start, levels):
    for sweep in range(ITERS):
        if sweep == 0:
            *parts, cross, places = left_product_first(start, cross)
            got = [swap(parts[at + 1], "var", Z_RINGS, mask) for at, mask in enumerate(MASKS)]
            total = parts[0]
        else:
            *parts, both, gram = left_partners(right_sum, squares, levels, cross, places)
            got = [swap(part, "var", Z_RINGS, mask) for part, mask in zip(parts, MASKS)]
            total = left_own(both, gram, cross, places)
        total = (total + got[0]) + (got[1] + got[2])
        total = ring_sum(total, "var", Y_RINGS)
        block = total[:, :QUARTER]
        blocks = [block] + [swap(block, "var", Z_RINGS, mask) for mask in MASKS]
        inverse = factor(total[:, QUARTER:], NG) if sweep else None
        left_sum, squares = assemble(inverse, blocks, places, Z_AT, 1, "assemble_left")
        squares = ring_sum(pair_sum(squares), "vox", X_RINGS)

        part, both, gram, left_shrunk = right_half(True, (left_sum, squares, levels), cross, places, 1)
        got = swap(part, "vox", CORE_PAIRS, 1)
        (total,) = right_half(False, (both, gram), cross, places, 0)
        total = ring_sum(total + got, "vox", X_RINGS)
        block = total[:, :HALF]
        got = swap(block, "vox", CORE_PAIRS, 1)
        inverse = factor(total[:, HALF:], NV)
        if sweep == ITERS - 1:
            left_dirs, left_terms = mix_left(inverse, left_shrunk)
            got, left_terms = lax.optimization_barrier((got, left_terms))
        blocks = [block, got]
        right_sum, squares = assemble(inverse, blocks, places, CORE_AT, 16, "assemble_right")
        squares = from_all(squares)
    right_shrunk, last = last_shrink(right_sum, squares, levels)
    last = from_all(last)
    deflated, right_dirs, strength = deflate(last, right_shrunk, left_terms, cross)
    return (deflated, left_dirs, right_dirs, strength.reshape(K))


def solution(mesh):
    in_specs = (P("vox", "var"), P(None, "var"), P())
    out_specs = (P("vox", "var"), P(None, "vox"), P(None, "var"), P())
    return jax.shard_map(
        per_device, mesh=mesh, in_specs=in_specs, out_specs=out_specs, check_vma=False
    )
```

```python
import math

import jax
import jax.numpy as jnp
from jax import lax
from jax.experimental import pallas as pl
from jax.experimental.pallas import tpu as pltpu
from jax.sharding import PartitionSpec as P

NV = 16384
NG = 24576
K = 32
ITERS = 2
ROWS = 2048
COLS = 1536
QUARTER = ROWS // 4
HALF = COLS // 2
BLOCK = 1024
LANES = 128
LEFT_ROWS = K * QUARTER // LANES
RIGHT_ROWS = K * HALF // LANES
GRAM_ROWS = K * K // LANES

EPSILON = 1e-06
F32 = jnp.float32
BF16 = jnp.bfloat16
NT = (((1,), (1,)), ((), ()))
NN = (((1,), (0,)), ((), ()))

X_RINGS = [[x * 2 + c for x in range(4)] for c in range(2)]
CORE_PAIRS = [[x * 2, x * 2 + 1] for x in range(4)]
Y_RINGS = [[y * 4 + z for y in range(4)] for z in range(4)]
Z_RINGS = [[y * 4 + z for z in range(4)] for y in range(4)]
MASKS = (1, 3, 2)

PARAMS = pltpu.CompilerParams(vmem_limit_bytes=24 * 2**20)
FIRST_PARAMS = pltpu.CompilerParams(vmem_limit_bytes=40 * 2**20)


def swap(value, axis, rings, mask):
    pairs = [(r[i], r[i ^ mask]) for r in rings for i in range(len(r))]
    return lax.ppermute(value, axis, pairs)


def ring_sum(value, axis, rings):
    got = [swap(value, axis, rings, mask) for mask in MASKS]
    return (value + got[0]) + (got[1] + got[2])


def from_all(value):
    return lax.all_to_all(value, "var", 0, 0)


def pair_sum(value):
    return value + swap(value, "vox", CORE_PAIRS, 1)


def dot(a, b, dims):
    return lax.dot_general(a, b, dims, preferred_element_type=F32)


def split2(x):
    high = x.astype(BF16)
    return high, (x - high.astype(F32)).astype(BF16)


def split3(x):
    high = x.astype(BF16)
    rest = x - high.astype(F32)
    middle = rest.astype(BF16)
    return high, middle, (rest - middle.astype(F32)).astype(BF16)


def mixed(matrix, values):
    high, middle, low = split3(matrix)
    left = jnp.concatenate([low, middle, high, middle, high, high], axis=1)
    high, middle, low = split3(values)
    return dot(left, jnp.concatenate([high, middle, low, high, middle, high], axis=0), NN)


def diagonal(width=LANES, offset=0):
    row = lax.broadcasted_iota(jnp.int32, (K, width), 0)
    lane = lax.broadcasted_iota(jnp.int32, (K, width), 1)
    return lane == row + offset


def to_column(row):
    return jnp.sum(jnp.where(diagonal(K), row, 0.0), axis=1, keepdims=True)


def to_row(column):
    return jnp.sum(jnp.where(diagonal(), column, 0.0), axis=0, keepdims=True)


def cross_gram(a, b):
    parts = dot(jnp.concatenate(split3(a), axis=0), jnp.concatenate(split3(b), axis=0), NT)
    rows = parts[:K] + (parts[K : 2 * K] + parts[2 * K :])
    return rows[:, :K] + (rows[:, K : 2 * K] + rows[:, 2 * K :])


def shrunk_of(values, squares, levels, side, count):
    squares = jnp.sum(squares, axis=0)
    thresholds = levels[side : side + 1, :].astype(F32) / 1024.0
    level = to_column(thresholds * jnp.sqrt(squares[:, :K] / count + EPSILON))
    return values - jnp.clip(values, -level, level)


def stack(ref, values):
    for at in range(values.shape[1] // LANES):
        ref[at * K : (at + 1) * K, :] = values[:, at * LANES : (at + 1) * LANES]


def unstacked(values):
    return jnp.concatenate([values[at : at + K] for at in range(0, values.shape[0], K)], axis=1)


def packed_gram(gram):
    return jnp.concatenate([gram[at : at + GRAM_ROWS] for at in range(0, K, GRAM_ROWS)], axis=1)


def unpacked_gram(packed):
    return jnp.concatenate([packed[:, at : at + K] for at in range(0, LANES, K)], axis=0)


def padded(small):
    return jnp.concatenate([small, jnp.zeros((K, LANES - small.shape[1]), F32)], axis=1)


def inverse_factor(gram, count):
    start = gram / count + jnp.where(diagonal(K), EPSILON, 0.0)
    start = jnp.concatenate(
        [jnp.where(diagonal(K), 1.0, 0.0), start, jnp.zeros((K, LANES - 2 * K), F32)], axis=1
    )
    blocks = [start[8 * b : 8 * b + 8] for b in range(4)]
    row = lax.broadcasted_iota(jnp.int32, (8, LANES), 0)
    pivots = []
    for panel in range(4):
        columns = [
            {
                b: jnp.broadcast_to(blocks[b][:, K + 8 * panel + t : K + 8 * panel + t + 1], (8, LANES))
                for b in range(panel, 4)
            }
            for t in range(8)
        ]
        pivot_of = jnp.ones((8, LANES), F32)
        for t in range(8):
            pivot = columns[t][panel][t : t + 1]
            pivot_of = jnp.where(row == t, pivot, pivot_of)
            inverse = 1.0 / pivot
            top = blocks[panel][t : t + 1]
            for b in range(panel, 4):
                factor = columns[t][b] * inverse
                if b == panel:
                    factor = jnp.where(row > t, factor, 0.0)
                columns[t][b] = factor
            for u in range(t + 1, 8):
                head = columns[u][panel][t : t + 1]
                for b in range(panel, 4):
                    columns[u][b] = columns[u][b] - columns[t][b] * head
            for b in range(panel, 4):
                blocks[b] = blocks[b] - columns[t][b] * top
        pivots.append(pivot_of)
    scale = 1.0 / jnp.sqrt(jnp.concatenate(pivots, axis=0))
    return (jnp.concatenate(blocks, axis=0) * scale)[:, :K]


Z_AT, CORE_AT = 0, 4


def left_product_first(right, cross):
    chunk = QUARTER // 2
    chunks = ROWS // chunk
    ahead = 6

    def kernel(right_hbm, cross_hbm, *refs):
        *outs, kept_ref, places_ref, right_ref, right_sem, sems = refs
        z = lax.rem(lax.axis_index("var"), 4)
        core = lax.rem(lax.axis_index("vox"), 2)
        places = [z] + [lax.bitwise_xor(z, jnp.int32(mask)) for mask in MASKS]

        def rows_of(at):
            first = places[at // 2] * QUARTER + (at % 2) * chunk
            return pl.ds(pl.multiple_of(first, chunk), chunk)

        def copy_of(at):
            return pltpu.make_async_copy(
                cross_hbm.at[rows_of(at), :], kept_ref.at[rows_of(at), :], sems.at[at]
            )

        right_copy = pltpu.make_async_copy(right_hbm, right_ref, right_sem)
        right_copy.start()
        for at in range(ahead):
            copy_of(at).start()
        for at, place in enumerate(places):
            places_ref[Z_AT + at] = place
        places_ref[CORE_AT] = core
        places_ref[CORE_AT + 1] = 1 - core
        places_ref[6] = 0
        places_ref[7] = 0
        right_copy.wait()
        both = jnp.concatenate(split2(right_ref[...]), axis=0)
        for quarter in range(4):
            for at in (2 * quarter, 2 * quarter + 1):
                copy_of(at).wait()
                if at + ahead < chunks:
                    copy_of(at + ahead).start()
            rows = pl.ds(pl.multiple_of(places[quarter] * QUARTER, QUARTER), QUARTER)
            stack(outs[quarter], left_terms_of(both, kept_ref[rows, :]))

    vmem = pl.BlockSpec(memory_space=pltpu.VMEM)
    hbm = pl.BlockSpec(memory_space=pltpu.HBM)
    return pl.pallas_call(
        kernel,
        in_specs=[hbm, hbm],
        out_specs=[vmem] * 5 + [pl.BlockSpec(memory_space=pltpu.SMEM)],
        out_shape=[jax.ShapeDtypeStruct((LEFT_ROWS, LANES), F32)] * 4
        + [jax.ShapeDtypeStruct((ROWS, COLS), F32), jax.ShapeDtypeStruct((8,), jnp.int32)],
        scratch_shapes=[
            pltpu.VMEM((K, COLS), F32),
            pltpu.SemaphoreType.DMA,
            pltpu.SemaphoreType.DMA((chunks,)),
        ],
        compiler_params=FIRST_PARAMS,
        name="left_product_first",
    )(right, cross)


def left_terms_of(both, block):
    high, low = split2(block)
    whole = dot(both, high, NT)
    return whole[:K] + (whole[K:] + dot(both[:K], low, NT))


def left_partners(right_sum, squares, levels, cross, places):
    def kernel(places_ref, right_ref, squares_ref, levels_ref, cross_ref, *refs):
        *outs, both_ref, gram_ref = refs
        step = pl.program_id(0)

        @pl.when(step == 0)
        def _():
            values = shrunk_of(right_ref[...], squares_ref[...], levels_ref[...], 1, NG)
            both_ref[...] = jnp.concatenate(split2(values), axis=0)
            gram_ref[...] = packed_gram(cross_gram(values, values))

        product = left_terms_of(both_ref[...], cross_ref[...])
        for at in range(3):

            @pl.when(step == at)
            def _():
                stack(outs[at], product)
                outs[at][LEFT_ROWS:, :] = gram_ref[...]

    whole = lambda shape: pl.BlockSpec(shape, lambda i, p: (0,) * len(shape))
    shapes = [((LEFT_ROWS + GRAM_ROWS, LANES), F32)] * 3 + [((2 * K, COLS), BF16), ((GRAM_ROWS, LANES), F32)]
    return pl.pallas_call(
        kernel,
        grid_spec=pltpu.PrefetchScalarGridSpec(
            num_scalar_prefetch=1,
            grid=(3,),
            in_specs=[whole((K, COLS)), whole((16, 1, LANES)), whole((2, K))]
            + [pl.BlockSpec((QUARTER, COLS), lambda i, p: (p[Z_AT + 1 + i], 0))],
            out_specs=[whole(shape) for shape, _ in shapes],
        ),
        out_shape=[jax.ShapeDtypeStruct(*shape) for shape in shapes],
        compiler_params=PARAMS,
        name="left_partners",
    )(places, right_sum, squares, levels, cross)


def left_own(both, gram, cross, places):
    def kernel(places_ref, both_ref, gram_ref, cross_ref, out_ref):
        stack(out_ref, left_terms_of(both_ref[...], cross_ref[...]))
        out_ref[LEFT_ROWS:, :] = gram_ref[...]

    whole = lambda shape: pl.BlockSpec(shape, lambda i, p: (0,) * len(shape))
    return pl.pallas_call(
        kernel,
        grid_spec=pltpu.PrefetchScalarGridSpec(
            num_scalar_prefetch=1,
            grid=(1,),
            in_specs=[whole((2 * K, COLS)), whole((GRAM_ROWS, LANES))]
            + [pl.BlockSpec((QUARTER, COLS), lambda i, p: (p[Z_AT], 0))],
            out_specs=whole((LEFT_ROWS + GRAM_ROWS, LANES)),
        ),
        out_shape=jax.ShapeDtypeStruct((LEFT_ROWS + GRAM_ROWS, LANES), F32),
        compiler_params=PARAMS,
        cost_estimate=pl.CostEstimate(flops=600_000_000, bytes_accessed=4_000_000, transcendentals=0),
        name="left_own",
    )(places, both, gram, cross)


def right_half(head, given, cross, places, at):
    def kernel(places_ref, *refs):
        if head:
            left_ref, squares_ref, levels_ref, cross_ref, out_ref, both_ref, gram_ref, shrunk_ref = refs

            values = shrunk_of(left_ref[...], squares_ref[...], levels_ref[...], 0, NV)
            shrunk_ref[...] = values
            both_ref[...] = jnp.concatenate(split2(values), axis=0)
            gram_ref[...] = packed_gram(cross_gram(values, values))
        else:
            both_ref, gram_ref, cross_ref, out_ref = refs
        high, low = split2(cross_ref[...])
        product = dot(both_ref[...], high, NN)
        stack(out_ref, product[:K] + (product[K:] + dot(both_ref[:K], low, NN)))
        out_ref[RIGHT_ROWS:, :] = gram_ref[...]

    whole = lambda shape: pl.BlockSpec(shape, lambda i, p: (0,) * len(shape))
    out_shape = [jax.ShapeDtypeStruct((RIGHT_ROWS + GRAM_ROWS, LANES), F32)]
    if head:
        out_shape += [
            jax.ShapeDtypeStruct((2 * K, ROWS), BF16),
            jax.ShapeDtypeStruct((GRAM_ROWS, LANES), F32),
            jax.ShapeDtypeStruct((K, ROWS), F32),
        ]
    return pl.pallas_call(
        kernel,
        grid_spec=pltpu.PrefetchScalarGridSpec(
            num_scalar_prefetch=1,
            grid=(1,),
            in_specs=[whole(g.shape) for g in given]
            + [pl.BlockSpec((ROWS, HALF), lambda i, p: (0, p[CORE_AT + at]))],
            out_specs=[whole(o.shape) for o in out_shape],
        ),
        out_shape=out_shape,
        compiler_params=PARAMS,
        cost_estimate=pl.CostEstimate(flops=1_200_000_000, bytes_accessed=8_000_000, transcendentals=0),
        name="right_half_head" if head else "right_half",
    )(places, *given, cross)


def factor(gram, count):
    def kernel(gram_ref, out_ref):
        out_ref[...] = padded(inverse_factor(unpacked_gram(gram_ref[...]), count))

    return pl.pallas_call(
        kernel,
        out_shape=jax.ShapeDtypeStruct((K, LANES), F32),
        compiler_params=PARAMS,
        cost_estimate=pl.CostEstimate(flops=10_000_000, bytes_accessed=8_000_000, transcendentals=0),
        name="factor",
    )(gram)


def assemble(inverse, blocks, places, start, copies, order):
    width = blocks[0].shape[0] * LANES // K
    n = len(blocks)

    def kernel(places_ref, *refs):
        if inverse is not None:
            inverse_ref, *refs = refs
        *ins, out_ref, squares_ref = refs
        total = jnp.zeros((K, 1), F32)
        for at, block in enumerate(ins):
            values = unstacked(block[...])
            if inverse is not None:
                values = mixed(inverse_ref[:, :K], values)
            out_ref[:, pl.ds(pl.multiple_of(places_ref[start + at] * width, width), width)] = values
            total = total + jnp.sum(values * values, axis=1, keepdims=True)
        squares_ref[...] = jnp.broadcast_to(to_row(total)[None], (copies, 1, LANES))

    args = blocks if inverse is None else [inverse, *blocks]
    vmem = pl.BlockSpec(memory_space=pltpu.VMEM)
    return pl.pallas_call(
        kernel,
        in_specs=[pl.BlockSpec(memory_space=pltpu.SMEM)] + [vmem] * len(args),
        out_specs=[vmem, vmem],
        out_shape=[
            jax.ShapeDtypeStruct((K, n * width), F32),
            jax.ShapeDtypeStruct((copies, 1, LANES), F32),
        ],
        compiler_params=PARAMS,
        name=order,
    )(places, *args)


def last_shrink(right_sum, squares, levels):
    def kernel(right_ref, squares_ref, levels_ref, shrunk_ref, out_ref):
        sums = right_ref[...]
        values = shrunk_of(sums, squares_ref[...], levels_ref[...], 1, NG)
        shrunk_ref[...] = values
        both = jnp.concatenate([cross_gram(values, values), cross_gram(sums, values)], axis=1)
        packed = jnp.concatenate([both[: K // 2], both[K // 2 :]], axis=1)
        out_ref[...] = jnp.broadcast_to(packed[None], (16, K // 2, LANES))

    return pl.pallas_call(
        kernel,
        out_shape=[
            jax.ShapeDtypeStruct((K, COLS), F32),
            jax.ShapeDtypeStruct((16, K // 2, LANES), F32),
        ],
        compiler_params=PARAMS,
        name="last_shrink",
    )(right_sum, squares, levels)


def mix_left(inverse, shrunk):
    def kernel(inverse_ref, shrunk_ref, out_ref, terms_ref):
        left = mixed(inverse_ref[:, :K], shrunk_ref[...])
        out_ref[...] = left
        high, middle, low = split3(left)
        terms_ref[...] = jnp.concatenate([high, high, middle, high, middle, low], axis=0).T

    return pl.pallas_call(
        kernel,
        out_shape=[
            jax.ShapeDtypeStruct((K, ROWS), F32),
            jax.ShapeDtypeStruct((ROWS, 6 * K), BF16),
        ],
        compiler_params=PARAMS,
        name="mix_left",
    )(inverse, shrunk)


def deflate(last, right_shrunk, left_terms, cross):
    def kernel(last_ref, shrunk_ref, left_ref, cross_ref, out_ref, right_ref, strength_ref, terms_ref):
        step = pl.program_id(0)

        @pl.when(step == 0)
        def _():
            packed = jnp.sum(last_ref[...], axis=0)
            last = jnp.concatenate([packed[:, : 2 * K], packed[:, 2 * K :]], axis=0)
            inverse = inverse_factor(last[:, :K], NG)
            right = mixed(inverse, shrunk_ref[...])
            right_ref[...] = right
            strength = jnp.sum(inverse * last[:, K:], axis=1, keepdims=True) / math.sqrt(NV * NG)
            strength_ref[...] = to_row(strength)[:, :K]
            high, middle, low = split3(right * (strength / math.sqrt(NV * NG)))
            terms_ref[...] = jnp.concatenate([high, middle, high, low, middle, high], axis=0)

        out_ref[...] = cross_ref[...] - dot(left_ref[...], terms_ref[...], NN)

    whole = lambda shape: pl.BlockSpec(shape, lambda i: (0,) * len(shape))
    return pl.pallas_call(
        kernel,
        grid=(ROWS // BLOCK,),
        in_specs=[
            whole((16, K // 2, LANES)),
            whole((K, COLS)),
            pl.BlockSpec((BLOCK, 6 * K), lambda i: (i, 0)),
            pl.BlockSpec((BLOCK, COLS), lambda i: (i, 0)),
        ],
        out_specs=[
            pl.BlockSpec((BLOCK, COLS), lambda i: (i, 0)),
            whole((K, COLS)),
            whole((1, K)),
        ],
        out_shape=[
            jax.ShapeDtypeStruct((ROWS, COLS), F32),
            jax.ShapeDtypeStruct((K, COLS), F32),
            jax.ShapeDtypeStruct((1, K), F32),
        ],
        scratch_shapes=[pltpu.VMEM((6 * K, COLS), BF16)],
        compiler_params=PARAMS,
        name="deflate",
    )(last, right_shrunk, left_terms, cross)


def per_device(cross, start, levels):
    for sweep in range(ITERS):
        if sweep == 0:
            *parts, cross, places = left_product_first(start, cross)
            got = [swap(parts[at + 1], "var", Z_RINGS, mask) for at, mask in enumerate(MASKS)]
            total = parts[0]
        else:
            *parts, both, gram = left_partners(right_sum, squares, levels, cross, places)
            got = [swap(part, "var", Z_RINGS, mask) for part, mask in zip(parts, MASKS)]
            total = left_own(both, gram, cross, places)
        total = (total + got[0]) + (got[1] + got[2])
        total = ring_sum(total, "var", Y_RINGS)
        block = total[:LEFT_ROWS]
        blocks = [block] + [swap(block, "var", Z_RINGS, mask) for mask in MASKS]
        inverse = factor(total[LEFT_ROWS:], NG) if sweep else None
        left_sum, squares = assemble(inverse, blocks, places, Z_AT, 1, "assemble_left")
        squares = ring_sum(pair_sum(squares), "vox", X_RINGS)

        part, both, gram, left_shrunk = right_half(True, (left_sum, squares, levels), cross, places, 1)
        got = swap(part, "vox", CORE_PAIRS, 1)
        (total,) = right_half(False, (both, gram), cross, places, 0)
        total = ring_sum(total + got, "vox", X_RINGS)
        block = total[:RIGHT_ROWS]
        got = swap(block, "vox", CORE_PAIRS, 1)
        inverse = factor(total[RIGHT_ROWS:], NV)
        if sweep == ITERS - 1:
            left_dirs, left_terms = mix_left(inverse, left_shrunk)
            got, left_terms = lax.optimization_barrier((got, left_terms))
        blocks = [block, got]
        right_sum, squares = assemble(inverse, blocks, places, CORE_AT, 16, "assemble_right")
        squares = from_all(squares)
    right_shrunk, last = last_shrink(right_sum, squares, levels)
    last = from_all(last)
    deflated, right_dirs, strength = deflate(last, right_shrunk, left_terms, cross)
    return (deflated, left_dirs, right_dirs, strength.reshape(K))


def solution(mesh):
    in_specs = (P("vox", "var"), P(None, "var"), P())
    out_specs = (P("vox", "var"), P(None, "vox"), P(None, "var"), P())
    return jax.shard_map(
        per_device, mesh=mesh, in_specs=in_specs, out_specs=out_specs, check_vma=False
    )
```

```python
import math

import jax
import jax.numpy as jnp
from jax import lax
from jax.experimental import pallas as pl
from jax.experimental.pallas import tpu as pltpu
from jax.sharding import PartitionSpec as P

NV = 16384
NG = 24576
K = 32
ITERS = 2
ROWS = 2048
COLS = 1536
QUARTER = ROWS // 4
HALF = COLS // 2
BLOCK = 1024
LANES = 128
LEFT_ROWS = K * QUARTER // LANES
RIGHT_ROWS = K * HALF // LANES
GRAM_ROWS = K * K // LANES

EPSILON = 1e-06
F32 = jnp.float32
BF16 = jnp.bfloat16
NT = (((1,), (1,)), ((), ()))
NN = (((1,), (0,)), ((), ()))

X_RINGS = [[x * 2 + c for x in range(4)] for c in range(2)]
CORE_PAIRS = [[x * 2, x * 2 + 1] for x in range(4)]
Y_RINGS = [[y * 4 + z for y in range(4)] for z in range(4)]
Z_RINGS = [[y * 4 + z for z in range(4)] for y in range(4)]
MASKS = (1, 3, 2)

PARAMS = pltpu.CompilerParams(vmem_limit_bytes=24 * 2**20)
FIRST_PARAMS = pltpu.CompilerParams(vmem_limit_bytes=40 * 2**20)


def swap(value, axis, rings, mask):
    pairs = [(r[i], r[i ^ mask]) for r in rings for i in range(len(r))]
    return lax.ppermute(value, axis, pairs)


def ring_sum(value, axis, rings):
    got = [swap(value, axis, rings, mask) for mask in MASKS]
    return (value + got[0]) + (got[1] + got[2])


def from_all(value):
    return lax.all_to_all(value, "var", 0, 0)


def pair_sum(value):
    return value + swap(value, "vox", CORE_PAIRS, 1)


def dot(a, b, dims):
    return lax.dot_general(a, b, dims, preferred_element_type=F32)


def split2(x):
    high = x.astype(BF16)
    return high, (x - high.astype(F32)).astype(BF16)


def split3(x):
    high = x.astype(BF16)
    rest = x - high.astype(F32)
    middle = rest.astype(BF16)
    return high, middle, (rest - middle.astype(F32)).astype(BF16)


def mixed(matrix, values):
    high, middle, low = split3(matrix)
    left = jnp.concatenate([low, middle, high, middle, high, high], axis=1)
    high, middle, low = split3(values)
    return dot(left, jnp.concatenate([high, middle, low, high, middle, high], axis=0), NN)


def diagonal(width=LANES, offset=0):
    row = lax.broadcasted_iota(jnp.int32, (K, width), 0)
    lane = lax.broadcasted_iota(jnp.int32, (K, width), 1)
    return lane == row + offset


def to_column(row):
    return jnp.sum(jnp.where(diagonal(K), row, 0.0), axis=1, keepdims=True)


def to_row(column):
    return jnp.sum(jnp.where(diagonal(), column, 0.0), axis=0, keepdims=True)


def cross_gram(a, b):
    parts = dot(jnp.concatenate(split3(a), axis=0), jnp.concatenate(split3(b), axis=0), NT)
    rows = parts[:K] + (parts[K : 2 * K] + parts[2 * K :])
    return rows[:, :K] + (rows[:, K : 2 * K] + rows[:, 2 * K :])


def shrunk_of(values, squares, levels, side, count):
    squares = jnp.sum(squares, axis=0)
    thresholds = levels[side : side + 1, :].astype(F32) / 1024.0
    level = to_column(thresholds * jnp.sqrt(squares[:, :K] / count + EPSILON))
    return values - jnp.clip(values, -level, level)


def stack(ref, values, first=0):
    for at in range(values.shape[1] // LANES):
        ref[first + at * K : first + (at + 1) * K, :] = values[:, at * LANES : (at + 1) * LANES]


def unstacked(values):
    return jnp.concatenate([values[at : at + K] for at in range(0, values.shape[0], K)], axis=1)


def packed_gram(gram):
    return jnp.concatenate([gram[at : at + GRAM_ROWS] for at in range(0, K, GRAM_ROWS)], axis=1)


def unpacked_gram(packed):
    return jnp.concatenate([packed[:, at : at + K] for at in range(0, LANES, K)], axis=0)


def padded(small):
    return jnp.concatenate([small, jnp.zeros((K, LANES - small.shape[1]), F32)], axis=1)


def inverse_factor(gram, count):
    start = gram / count + jnp.where(diagonal(K), EPSILON, 0.0)
    start = jnp.concatenate(
        [jnp.where(diagonal(K), 1.0, 0.0), start, jnp.zeros((K, LANES - 2 * K), F32)], axis=1
    )
    blocks = [start[8 * b : 8 * b + 8] for b in range(4)]
    row = lax.broadcasted_iota(jnp.int32, (8, LANES), 0)
    pivots = []
    for panel in range(4):
        columns = [
            {
                b: jnp.broadcast_to(blocks[b][:, K + 8 * panel + t : K + 8 * panel + t + 1], (8, LANES))
                for b in range(panel, 4)
            }
            for t in range(8)
        ]
        pivot_of = jnp.ones((8, LANES), F32)
        for t in range(8):
            pivot = columns[t][panel][t : t + 1]
            pivot_of = jnp.where(row == t, pivot, pivot_of)
            inverse = 1.0 / pivot
            top = blocks[panel][t : t + 1]
            for b in range(panel, 4):
                factor = columns[t][b] * inverse
                if b == panel:
                    factor = jnp.where(row > t, factor, 0.0)
                columns[t][b] = factor
            for u in range(t + 1, 8):
                head = columns[u][panel][t : t + 1]
                for b in range(panel, 4):
                    columns[u][b] = columns[u][b] - columns[t][b] * head
            for b in range(panel, 4):
                blocks[b] = blocks[b] - columns[t][b] * top
        pivots.append(pivot_of)
    scale = 1.0 / jnp.sqrt(jnp.concatenate(pivots, axis=0))
    return (jnp.concatenate(blocks, axis=0) * scale)[:, :K]


Z_AT, CORE_AT = 0, 4


def left_product_first(right, cross):
    chunk = QUARTER // 2
    chunks = ROWS // chunk

    def kernel(right_hbm, cross_hbm, *refs):
        *outs, kept_ref, places_ref, right_ref, right_sem, sems = refs
        z = lax.rem(lax.axis_index("var"), 4)
        core = lax.rem(lax.axis_index("vox"), 2)
        places = [z] + [lax.bitwise_xor(z, jnp.int32(mask)) for mask in MASKS]

        def rows_of(at):
            first = places[at // 2] * QUARTER + (at % 2) * chunk
            return pl.ds(pl.multiple_of(first, chunk), chunk)

        def copy_of(at):
            return pltpu.make_async_copy(
                cross_hbm.at[rows_of(at), :], kept_ref.at[rows_of(at), :], sems.at[at]
            )

        right_copy = pltpu.make_async_copy(right_hbm, right_ref, right_sem)
        right_copy.start()
        for at in range(chunks):
            copy_of(at).start()
        for at, place in enumerate(places):
            places_ref[Z_AT + at] = place
        places_ref[CORE_AT] = core
        places_ref[CORE_AT + 1] = 1 - core
        places_ref[6] = 0
        places_ref[7] = 0
        right_copy.wait()
        both = jnp.concatenate(split2(right_ref[...]), axis=0)
        for at in range(chunks):
            copy_of(at).wait()
            product = left_terms_of(both, kept_ref[rows_of(at), :])
            stack(outs[at // 2], product, at % 2 * (LEFT_ROWS // 2))

    vmem = pl.BlockSpec(memory_space=pltpu.VMEM)
    hbm = pl.BlockSpec(memory_space=pltpu.HBM)
    return pl.pallas_call(
        kernel,
        in_specs=[hbm, hbm],
        out_specs=[vmem] * 5 + [pl.BlockSpec(memory_space=pltpu.SMEM)],
        out_shape=[jax.ShapeDtypeStruct((LEFT_ROWS, LANES), F32)] * 4
        + [jax.ShapeDtypeStruct((ROWS, COLS), F32), jax.ShapeDtypeStruct((8,), jnp.int32)],
        scratch_shapes=[
            pltpu.VMEM((K, COLS), F32),
            pltpu.SemaphoreType.DMA,
            pltpu.SemaphoreType.DMA((chunks,)),
        ],
        compiler_params=FIRST_PARAMS,
        name="left_product_first",
    )(right, cross)


def left_terms_of(both, block):
    high, low = split2(block)
    whole = dot(both, high, NT)
    return whole[:K] + (whole[K:] + dot(both[:K], low, NT))


def left_partners(right_sum, squares, levels, cross, places):
    def kernel(places_ref, right_ref, squares_ref, levels_ref, cross_ref, *refs):
        *outs, both_ref, gram_ref = refs
        step = pl.program_id(0)

        @pl.when(step == 0)
        def _():
            values = shrunk_of(right_ref[...], squares_ref[...], levels_ref[...], 1, NG)
            both_ref[...] = jnp.concatenate(split2(values), axis=0)
            gram_ref[...] = packed_gram(cross_gram(values, values))

        product = left_terms_of(both_ref[...], cross_ref[...])
        for at in range(3):

            @pl.when(step == at)
            def _():
                stack(outs[at], product)
                outs[at][LEFT_ROWS:, :] = gram_ref[...]

    whole = lambda shape: pl.BlockSpec(shape, lambda i, p: (0,) * len(shape))
    shapes = [((LEFT_ROWS + GRAM_ROWS, LANES), F32)] * 3 + [((2 * K, COLS), BF16), ((GRAM_ROWS, LANES), F32)]
    return pl.pallas_call(
        kernel,
        grid_spec=pltpu.PrefetchScalarGridSpec(
            num_scalar_prefetch=1,
            grid=(3,),
            in_specs=[whole((K, COLS)), whole((16, 1, LANES)), whole((2, K))]
            + [pl.BlockSpec((QUARTER, COLS), lambda i, p: (p[Z_AT + 1 + i], 0))],
            out_specs=[whole(shape) for shape, _ in shapes],
        ),
        out_shape=[jax.ShapeDtypeStruct(*shape) for shape in shapes],
        compiler_params=PARAMS,
        name="left_partners",
    )(places, right_sum, squares, levels, cross)


def left_own(both, gram, cross, places):
    def kernel(places_ref, both_ref, gram_ref, cross_ref, out_ref):
        stack(out_ref, left_terms_of(both_ref[...], cross_ref[...]))
        out_ref[LEFT_ROWS:, :] = gram_ref[...]

    whole = lambda shape: pl.BlockSpec(shape, lambda i, p: (0,) * len(shape))
    return pl.pallas_call(
        kernel,
        grid_spec=pltpu.PrefetchScalarGridSpec(
            num_scalar_prefetch=1,
            grid=(1,),
            in_specs=[whole((2 * K, COLS)), whole((GRAM_ROWS, LANES))]
            + [pl.BlockSpec((QUARTER, COLS), lambda i, p: (p[Z_AT], 0))],
            out_specs=whole((LEFT_ROWS + GRAM_ROWS, LANES)),
        ),
        out_shape=jax.ShapeDtypeStruct((LEFT_ROWS + GRAM_ROWS, LANES), F32),
        compiler_params=PARAMS,
        cost_estimate=pl.CostEstimate(flops=600_000_000, bytes_accessed=4_000_000, transcendentals=0),
        name="left_own",
    )(places, both, gram, cross)


def right_half(head, given, cross, places, at):
    def kernel(places_ref, *refs):
        if head:
            left_ref, squares_ref, levels_ref, cross_ref, out_ref, both_ref, gram_ref, shrunk_ref = refs

            values = shrunk_of(left_ref[...], squares_ref[...], levels_ref[...], 0, NV)
            shrunk_ref[...] = values
            both_ref[...] = jnp.concatenate(split2(values), axis=0)
            gram_ref[...] = packed_gram(cross_gram(values, values))
        else:
            both_ref, gram_ref, cross_ref, out_ref = refs
        high, low = split2(cross_ref[...])
        product = dot(both_ref[...], high, NN)
        stack(out_ref, product[:K] + (product[K:] + dot(both_ref[:K], low, NN)))
        out_ref[RIGHT_ROWS:, :] = gram_ref[...]

    whole = lambda shape: pl.BlockSpec(shape, lambda i, p: (0,) * len(shape))
    out_shape = [jax.ShapeDtypeStruct((RIGHT_ROWS + GRAM_ROWS, LANES), F32)]
    if head:
        out_shape += [
            jax.ShapeDtypeStruct((2 * K, ROWS), BF16),
            jax.ShapeDtypeStruct((GRAM_ROWS, LANES), F32),
            jax.ShapeDtypeStruct((K, ROWS), F32),
        ]
    return pl.pallas_call(
        kernel,
        grid_spec=pltpu.PrefetchScalarGridSpec(
            num_scalar_prefetch=1,
            grid=(1,),
            in_specs=[whole(g.shape) for g in given]
            + [pl.BlockSpec((ROWS, HALF), lambda i, p: (0, p[CORE_AT + at]))],
            out_specs=[whole(o.shape) for o in out_shape],
        ),
        out_shape=out_shape,
        compiler_params=PARAMS,
        cost_estimate=pl.CostEstimate(flops=1_200_000_000, bytes_accessed=8_000_000, transcendentals=0),
        name="right_half_head" if head else "right_half",
    )(places, *given, cross)


def factor(gram, count):
    def kernel(gram_ref, out_ref):
        out_ref[...] = padded(inverse_factor(unpacked_gram(gram_ref[...]), count))

    return pl.pallas_call(
        kernel,
        out_shape=jax.ShapeDtypeStruct((K, LANES), F32),
        compiler_params=PARAMS,
        cost_estimate=pl.CostEstimate(flops=10_000_000, bytes_accessed=8_000_000, transcendentals=0),
        name="factor",
    )(gram)


def assemble(inverse, blocks, places, start, copies, order):
    width = blocks[0].shape[0] * LANES // K
    n = len(blocks)

    def kernel(places_ref, *refs):
        if inverse is not None:
            inverse_ref, *refs = refs
        *ins, out_ref, squares_ref = refs
        total = jnp.zeros((K, 1), F32)
        for at, block in enumerate(ins):
            values = unstacked(block[...])
            if inverse is not None:
                values = mixed(inverse_ref[:, :K], values)
            out_ref[:, pl.ds(pl.multiple_of(places_ref[start + at] * width, width), width)] = values
            total = total + jnp.sum(values * values, axis=1, keepdims=True)
        squares_ref[...] = jnp.broadcast_to(to_row(total)[None], (copies, 1, LANES))

    args = blocks if inverse is None else [inverse, *blocks]
    vmem = pl.BlockSpec(memory_space=pltpu.VMEM)
    return pl.pallas_call(
        kernel,
        in_specs=[pl.BlockSpec(memory_space=pltpu.SMEM)] + [vmem] * len(args),
        out_specs=[vmem, vmem],
        out_shape=[
            jax.ShapeDtypeStruct((K, n * width), F32),
            jax.ShapeDtypeStruct((copies, 1, LANES), F32),
        ],
        compiler_params=PARAMS,
        name=order,
    )(places, *args)


def last_shrink(right_sum, squares, levels):
    def kernel(right_ref, squares_ref, levels_ref, shrunk_ref, out_ref):
        sums = right_ref[...]
        values = shrunk_of(sums, squares_ref[...], levels_ref[...], 1, NG)
        shrunk_ref[...] = values
        both = jnp.concatenate([cross_gram(values, values), cross_gram(sums, values)], axis=1)
        packed = jnp.concatenate([both[: K // 2], both[K // 2 :]], axis=1)
        out_ref[...] = jnp.broadcast_to(packed[None], (16, K // 2, LANES))

    return pl.pallas_call(
        kernel,
        out_shape=[
            jax.ShapeDtypeStruct((K, COLS), F32),
            jax.ShapeDtypeStruct((16, K // 2, LANES), F32),
        ],
        compiler_params=PARAMS,
        name="last_shrink",
    )(right_sum, squares, levels)


def mix_left(inverse, shrunk):
    def kernel(inverse_ref, shrunk_ref, out_ref, terms_ref):
        left = mixed(inverse_ref[:, :K], shrunk_ref[...])
        out_ref[...] = left
        high, middle, low = split3(left)
        terms_ref[...] = jnp.concatenate([high, high, middle, high, middle, low], axis=0).T

    return pl.pallas_call(
        kernel,
        out_shape=[
            jax.ShapeDtypeStruct((K, ROWS), F32),
            jax.ShapeDtypeStruct((ROWS, 6 * K), BF16),
        ],
        compiler_params=PARAMS,
        name="mix_left",
    )(inverse, shrunk)


def deflate(last, right_shrunk, left_terms, cross):
    def kernel(last_ref, shrunk_ref, left_ref, cross_ref, out_ref, right_ref, strength_ref, terms_ref):
        step = pl.program_id(0)

        @pl.when(step == 0)
        def _():
            packed = jnp.sum(last_ref[...], axis=0)
            last = jnp.concatenate([packed[:, : 2 * K], packed[:, 2 * K :]], axis=0)
            inverse = inverse_factor(last[:, :K], NG)
            right = mixed(inverse, shrunk_ref[...])
            right_ref[...] = right
            strength = jnp.sum(inverse * last[:, K:], axis=1, keepdims=True) / math.sqrt(NV * NG)
            strength_ref[...] = to_row(strength)[:, :K]
            high, middle, low = split3(right * (strength / math.sqrt(NV * NG)))
            terms_ref[...] = jnp.concatenate([high, middle, high, low, middle, high], axis=0)

        out_ref[...] = cross_ref[...] - dot(left_ref[...], terms_ref[...], NN)

    whole = lambda shape: pl.BlockSpec(shape, lambda i: (0,) * len(shape))
    return pl.pallas_call(
        kernel,
        grid=(ROWS // BLOCK,),
        in_specs=[
            whole((16, K // 2, LANES)),
            whole((K, COLS)),
            pl.BlockSpec((BLOCK, 6 * K), lambda i: (i, 0)),
            pl.BlockSpec((BLOCK, COLS), lambda i: (i, 0)),
        ],
        out_specs=[
            pl.BlockSpec((BLOCK, COLS), lambda i: (i, 0)),
            whole((K, COLS)),
            whole((1, K)),
        ],
        out_shape=[
            jax.ShapeDtypeStruct((ROWS, COLS), F32),
            jax.ShapeDtypeStruct((K, COLS), F32),
            jax.ShapeDtypeStruct((1, K), F32),
        ],
        scratch_shapes=[pltpu.VMEM((6 * K, COLS), BF16)],
        compiler_params=PARAMS,
        name="deflate",
    )(last, right_shrunk, left_terms, cross)


def per_device(cross, start, levels):
    for sweep in range(ITERS):
        if sweep == 0:
            *parts, cross, places = left_product_first(start, cross)
            got = [swap(parts[at + 1], "var", Z_RINGS, mask) for at, mask in enumerate(MASKS)]
            total = parts[0]
        else:
            *parts, both, gram = left_partners(right_sum, squares, levels, cross, places)
            got = [swap(part, "var", Z_RINGS, mask) for part, mask in zip(parts, MASKS)]
            total = left_own(both, gram, cross, places)
        total = (total + got[0]) + (got[1] + got[2])
        total = ring_sum(total, "var", Y_RINGS)
        block = total[:LEFT_ROWS]
        blocks = [block] + [swap(block, "var", Z_RINGS, mask) for mask in MASKS]
        inverse = factor(total[LEFT_ROWS:], NG) if sweep else None
        left_sum, squares = assemble(inverse, blocks, places, Z_AT, 1, "assemble_left")
        squares = ring_sum(pair_sum(squares), "vox", X_RINGS)

        part, both, gram, left_shrunk = right_half(True, (left_sum, squares, levels), cross, places, 1)
        got = swap(part, "vox", CORE_PAIRS, 1)
        (total,) = right_half(False, (both, gram), cross, places, 0)
        total = ring_sum(total + got, "vox", X_RINGS)
        block = total[:RIGHT_ROWS]
        got = swap(block, "vox", CORE_PAIRS, 1)
        inverse = factor(total[RIGHT_ROWS:], NV)
        if sweep == ITERS - 1:
            left_dirs, left_terms = mix_left(inverse, left_shrunk)
            got, left_terms = lax.optimization_barrier((got, left_terms))
        blocks = [block, got]
        right_sum, squares = assemble(inverse, blocks, places, CORE_AT, 16, "assemble_right")
        squares = from_all(squares)
    right_shrunk, last = last_shrink(right_sum, squares, levels)
    last = from_all(last)
    deflated, right_dirs, strength = deflate(last, right_shrunk, left_terms, cross)
    return (deflated, left_dirs, right_dirs, strength.reshape(K))


def solution(mesh):
    in_specs = (P("vox", "var"), P(None, "var"), P())
    out_specs = (P("vox", "var"), P(None, "vox"), P(None, "var"), P())
    return jax.shard_map(
        per_device, mesh=mesh, in_specs=in_specs, out_specs=out_specs, check_vma=False
    )
```

```python
import math

import jax
import jax.numpy as jnp
from jax import lax
from jax.experimental import pallas as pl
from jax.experimental.pallas import tpu as pltpu
from jax.sharding import PartitionSpec as P

NV = 16384
NG = 24576
K = 32
ITERS = 2
ROWS = 2048
COLS = 1536
QUARTER = ROWS // 4
HALF = COLS // 2
BLOCK = 512
LANES = 128
LEFT_ROWS = K * QUARTER // LANES
RIGHT_ROWS = K * HALF // LANES
GRAM_ROWS = K * K // LANES

EPSILON = 1e-06
F32 = jnp.float32
BF16 = jnp.bfloat16
NT = (((1,), (1,)), ((), ()))
NN = (((1,), (0,)), ((), ()))

X_RINGS = [[x * 2 + c for x in range(4)] for c in range(2)]
CORE_PAIRS = [[x * 2, x * 2 + 1] for x in range(4)]
Y_RINGS = [[y * 4 + z for y in range(4)] for z in range(4)]
Z_RINGS = [[y * 4 + z for z in range(4)] for y in range(4)]
MASKS = (1, 3, 2)

PARAMS = pltpu.CompilerParams(vmem_limit_bytes=24 * 2**20)
FIRST_PARAMS = pltpu.CompilerParams(vmem_limit_bytes=40 * 2**20)


def swap(value, axis, rings, mask):
    pairs = [(r[i], r[i ^ mask]) for r in rings for i in range(len(r))]
    return lax.ppermute(value, axis, pairs)


def ring_sum(value, axis, rings):
    got = [swap(value, axis, rings, mask) for mask in MASKS]
    return (value + got[0]) + (got[1] + got[2])


def from_all(value):
    return lax.all_to_all(value, "var", 0, 0)


def pair_sum(value):
    return value + swap(value, "vox", CORE_PAIRS, 1)


def dot(a, b, dims):
    return lax.dot_general(a, b, dims, preferred_element_type=F32)


def split2(x):
    high = x.astype(BF16)
    return high, (x - high.astype(F32)).astype(BF16)


def split3(x):
    high = x.astype(BF16)
    rest = x - high.astype(F32)
    middle = rest.astype(BF16)
    return high, middle, (rest - middle.astype(F32)).astype(BF16)


def mixed(matrix, values):
    high, middle, low = split3(matrix)
    left = jnp.concatenate([low, middle, high, middle, high, high], axis=1)
    high, middle, low = split3(values)
    return dot(left, jnp.concatenate([high, middle, low, high, middle, high], axis=0), NN)


def diagonal(width=LANES, offset=0):
    row = lax.broadcasted_iota(jnp.int32, (K, width), 0)
    lane = lax.broadcasted_iota(jnp.int32, (K, width), 1)
    return lane == row + offset


def to_column(row):
    return jnp.sum(jnp.where(diagonal(K), row, 0.0), axis=1, keepdims=True)


def to_row(column):
    return jnp.sum(jnp.where(diagonal(), column, 0.0), axis=0, keepdims=True)


def cross_gram(a, b):
    parts = dot(jnp.concatenate(split3(a), axis=0), jnp.concatenate(split3(b), axis=0), NT)
    rows = parts[:K] + (parts[K : 2 * K] + parts[2 * K :])
    return rows[:, :K] + (rows[:, K : 2 * K] + rows[:, 2 * K :])


def shrunk_of(values, squares, levels, side, count):
    squares = jnp.sum(squares, axis=0)
    thresholds = levels[side : side + 1, :].astype(F32) / 1024.0
    level = to_column(thresholds * jnp.sqrt(squares[:, :K] / count + EPSILON))
    return values - jnp.clip(values, -level, level)


def stack(ref, values):
    for at in range(values.shape[1] // LANES):
        ref[at * K : (at + 1) * K, :] = values[:, at * LANES : (at + 1) * LANES]


def unstacked(values):
    return jnp.concatenate([values[at : at + K] for at in range(0, values.shape[0], K)], axis=1)


def packed_gram(gram):
    return jnp.concatenate([gram[at : at + GRAM_ROWS] for at in range(0, K, GRAM_ROWS)], axis=1)


def unpacked_gram(packed):
    return jnp.concatenate([packed[:, at : at + K] for at in range(0, LANES, K)], axis=0)


def padded(small):
    return jnp.concatenate([small, jnp.zeros((K, LANES - small.shape[1]), F32)], axis=1)


def inverse_factor(gram, count):
    start = gram / count + jnp.where(diagonal(K), EPSILON, 0.0)
    start = jnp.concatenate(
        [jnp.where(diagonal(K), 1.0, 0.0), start, jnp.zeros((K, LANES - 2 * K), F32)], axis=1
    )
    blocks = [start[8 * b : 8 * b + 8] for b in range(4)]
    row = lax.broadcasted_iota(jnp.int32, (8, LANES), 0)
    pivots = []
    for panel in range(4):
        columns = [
            {
                b: jnp.broadcast_to(blocks[b][:, K + 8 * panel + t : K + 8 * panel + t + 1], (8, LANES))
                for b in range(panel, 4)
            }
            for t in range(8)
        ]
        pivot_of = jnp.ones((8, LANES), F32)
        for t in range(8):
            pivot = columns[t][panel][t : t + 1]
            pivot_of = jnp.where(row == t, pivot, pivot_of)
            inverse = 1.0 / pivot
            top = blocks[panel][t : t + 1]
            for b in range(panel, 4):
                factor = columns[t][b] * inverse
                if b == panel:
                    factor = jnp.where(row > t, factor, 0.0)
                columns[t][b] = factor
            for u in range(t + 1, 8):
                head = columns[u][panel][t : t + 1]
                for b in range(panel, 4):
                    columns[u][b] = columns[u][b] - columns[t][b] * head
            for b in range(panel, 4):
                blocks[b] = blocks[b] - columns[t][b] * top
        pivots.append(pivot_of)
    scale = 1.0 / jnp.sqrt(jnp.concatenate(pivots, axis=0))
    return (jnp.concatenate(blocks, axis=0) * scale)[:, :K]


Z_AT, CORE_AT = 0, 4


def left_product_first(right, cross):
    chunk = QUARTER // 2
    chunks = ROWS // chunk
    ahead = 6

    def kernel(right_hbm, cross_hbm, *refs):
        *outs, kept_ref, places_ref, right_ref, right_sem, sems = refs
        z = lax.rem(lax.axis_index("var"), 4)
        core = lax.rem(lax.axis_index("vox"), 2)
        places = [z] + [lax.bitwise_xor(z, jnp.int32(mask)) for mask in MASKS]

        def rows_of(at):
            first = places[at // 2] * QUARTER + (at % 2) * chunk
            return pl.ds(pl.multiple_of(first, chunk), chunk)

        def copy_of(at):
            return pltpu.make_async_copy(
                cross_hbm.at[rows_of(at), :], kept_ref.at[rows_of(at), :], sems.at[at]
            )

        right_copy = pltpu.make_async_copy(right_hbm, right_ref, right_sem)
        right_copy.start()
        for at in range(ahead):
            copy_of(at).start()
        for at, place in enumerate(places):
            places_ref[Z_AT + at] = place
        places_ref[CORE_AT] = core
        places_ref[CORE_AT + 1] = 1 - core
        places_ref[6] = 0
        places_ref[7] = 0
        right_copy.wait()
        both = jnp.concatenate(split2(right_ref[...]), axis=0)
        for quarter in range(4):
            for at in (2 * quarter, 2 * quarter + 1):
                copy_of(at).wait()
                if at + ahead < chunks:
                    copy_of(at + ahead).start()
            rows = pl.ds(pl.multiple_of(places[quarter] * QUARTER, QUARTER), QUARTER)
            stack(outs[quarter], left_terms_of(both, kept_ref[rows, :]))

    vmem = pl.BlockSpec(memory_space=pltpu.VMEM)
    hbm = pl.BlockSpec(memory_space=pltpu.HBM)
    return pl.pallas_call(
        kernel,
        in_specs=[hbm, hbm],
        out_specs=[vmem] * 5 + [pl.BlockSpec(memory_space=pltpu.SMEM)],
        out_shape=[jax.ShapeDtypeStruct((LEFT_ROWS, LANES), F32)] * 4
        + [jax.ShapeDtypeStruct((ROWS, COLS), F32), jax.ShapeDtypeStruct((8,), jnp.int32)],
        scratch_shapes=[
            pltpu.VMEM((K, COLS), F32),
            pltpu.SemaphoreType.DMA,
            pltpu.SemaphoreType.DMA((chunks,)),
        ],
        compiler_params=FIRST_PARAMS,
        name="left_product_first",
    )(right, cross)


def left_terms_of(both, block):
    high, low = split2(block)
    whole = dot(both, high, NT)
    return whole[:K] + (whole[K:] + dot(both[:K], low, NT))


def left_partners(right_sum, squares, levels, cross, places):
    def kernel(places_ref, right_ref, squares_ref, levels_ref, cross_ref, *refs):
        *outs, both_ref, gram_ref = refs
        step = pl.program_id(0)

        @pl.when(step == 0)
        def _():
            values = shrunk_of(right_ref[...], squares_ref[...], levels_ref[...], 1, NG)
            both_ref[...] = jnp.concatenate(split2(values), axis=0)
            gram_ref[...] = packed_gram(cross_gram(values, values))

        product = left_terms_of(both_ref[...], cross_ref[...])
        for at in range(3):

            @pl.when(step == at)
            def _():
                stack(outs[at], product)
                outs[at][LEFT_ROWS:, :] = gram_ref[...]

    whole = lambda shape: pl.BlockSpec(shape, lambda i, p: (0,) * len(shape))
    shapes = [((LEFT_ROWS + GRAM_ROWS, LANES), F32)] * 3 + [((2 * K, COLS), BF16), ((GRAM_ROWS, LANES), F32)]
    return pl.pallas_call(
        kernel,
        grid_spec=pltpu.PrefetchScalarGridSpec(
            num_scalar_prefetch=1,
            grid=(3,),
            in_specs=[whole((K, COLS)), whole((16, 1, LANES)), whole((2, K))]
            + [pl.BlockSpec((QUARTER, COLS), lambda i, p: (p[Z_AT + 1 + i], 0))],
            out_specs=[whole(shape) for shape, _ in shapes],
        ),
        out_shape=[jax.ShapeDtypeStruct(*shape) for shape in shapes],
        compiler_params=PARAMS,
        name="left_partners",
    )(places, right_sum, squares, levels, cross)


def left_own(both, gram, cross, places):
    def kernel(places_ref, both_ref, gram_ref, cross_ref, out_ref):
        stack(out_ref, left_terms_of(both_ref[...], cross_ref[...]))
        out_ref[LEFT_ROWS:, :] = gram_ref[...]

    whole = lambda shape: pl.BlockSpec(shape, lambda i, p: (0,) * len(shape))
    return pl.pallas_call(
        kernel,
        grid_spec=pltpu.PrefetchScalarGridSpec(
            num_scalar_prefetch=1,
            grid=(1,),
            in_specs=[whole((2 * K, COLS)), whole((GRAM_ROWS, LANES))]
            + [pl.BlockSpec((QUARTER, COLS), lambda i, p: (p[Z_AT], 0))],
            out_specs=whole((LEFT_ROWS + GRAM_ROWS, LANES)),
        ),
        out_shape=jax.ShapeDtypeStruct((LEFT_ROWS + GRAM_ROWS, LANES), F32),
        compiler_params=PARAMS,
        cost_estimate=pl.CostEstimate(flops=600_000_000, bytes_accessed=4_000_000, transcendentals=0),
        name="left_own",
    )(places, both, gram, cross)


def right_half(head, given, cross, places, at):
    def kernel(places_ref, *refs):
        if head:
            left_ref, squares_ref, levels_ref, cross_ref, out_ref, both_ref, gram_ref, shrunk_ref = refs

            values = shrunk_of(left_ref[...], squares_ref[...], levels_ref[...], 0, NV)
            shrunk_ref[...] = values
            both_ref[...] = jnp.concatenate(split2(values), axis=0)
            gram_ref[...] = packed_gram(cross_gram(values, values))
        else:
            both_ref, gram_ref, cross_ref, out_ref = refs
        high, low = split2(cross_ref[...])
        product = dot(both_ref[...], high, NN)
        stack(out_ref, product[:K] + (product[K:] + dot(both_ref[:K], low, NN)))
        out_ref[RIGHT_ROWS:, :] = gram_ref[...]

    whole = lambda shape: pl.BlockSpec(shape, lambda i, p: (0,) * len(shape))
    out_shape = [jax.ShapeDtypeStruct((RIGHT_ROWS + GRAM_ROWS, LANES), F32)]
    if head:
        out_shape += [
            jax.ShapeDtypeStruct((2 * K, ROWS), BF16),
            jax.ShapeDtypeStruct((GRAM_ROWS, LANES), F32),
            jax.ShapeDtypeStruct((K, ROWS), F32),
        ]
    return pl.pallas_call(
        kernel,
        grid_spec=pltpu.PrefetchScalarGridSpec(
            num_scalar_prefetch=1,
            grid=(1,),
            in_specs=[whole(g.shape) for g in given]
            + [pl.BlockSpec((ROWS, HALF), lambda i, p: (0, p[CORE_AT + at]))],
            out_specs=[whole(o.shape) for o in out_shape],
        ),
        out_shape=out_shape,
        compiler_params=PARAMS,
        cost_estimate=pl.CostEstimate(flops=1_200_000_000, bytes_accessed=8_000_000, transcendentals=0),
        name="right_half_head" if head else "right_half",
    )(places, *given, cross)


def factor(gram, count):
    def kernel(gram_ref, out_ref):
        out_ref[...] = padded(inverse_factor(unpacked_gram(gram_ref[...]), count))

    return pl.pallas_call(
        kernel,
        out_shape=jax.ShapeDtypeStruct((K, LANES), F32),
        compiler_params=PARAMS,
        cost_estimate=pl.CostEstimate(flops=10_000_000, bytes_accessed=8_000_000, transcendentals=0),
        name="factor",
    )(gram)


def assemble(inverse, blocks, places, start, copies, order):
    width = blocks[0].shape[0] * LANES // K
    n = len(blocks)

    def kernel(places_ref, *refs):
        if inverse is not None:
            inverse_ref, *refs = refs
        *ins, out_ref, squares_ref = refs
        total = jnp.zeros((K, 1), F32)
        for at, block in enumerate(ins):
            values = unstacked(block[...])
            if inverse is not None:
                values = mixed(inverse_ref[:, :K], values)
            out_ref[:, pl.ds(pl.multiple_of(places_ref[start + at] * width, width), width)] = values
            total = total + jnp.sum(values * values, axis=1, keepdims=True)
        squares_ref[...] = jnp.broadcast_to(to_row(total)[None], (copies, 1, LANES))

    args = blocks if inverse is None else [inverse, *blocks]
    vmem = pl.BlockSpec(memory_space=pltpu.VMEM)
    return pl.pallas_call(
        kernel,
        in_specs=[pl.BlockSpec(memory_space=pltpu.SMEM)] + [vmem] * len(args),
        out_specs=[vmem, vmem],
        out_shape=[
            jax.ShapeDtypeStruct((K, n * width), F32),
            jax.ShapeDtypeStruct((copies, 1, LANES), F32),
        ],
        compiler_params=PARAMS,
        name=order,
    )(places, *args)


def last_shrink(right_sum, squares, levels):
    def kernel(right_ref, squares_ref, levels_ref, shrunk_ref, out_ref):
        sums = right_ref[...]
        values = shrunk_of(sums, squares_ref[...], levels_ref[...], 1, NG)
        shrunk_ref[...] = values
        both = jnp.concatenate([cross_gram(values, values), cross_gram(sums, values)], axis=1)
        packed = jnp.concatenate([both[: K // 2], both[K // 2 :]], axis=1)
        out_ref[...] = jnp.broadcast_to(packed[None], (16, K // 2, LANES))

    return pl.pallas_call(
        kernel,
        out_shape=[
            jax.ShapeDtypeStruct((K, COLS), F32),
            jax.ShapeDtypeStruct((16, K // 2, LANES), F32),
        ],
        compiler_params=PARAMS,
        name="last_shrink",
    )(right_sum, squares, levels)


def mix_left(inverse, shrunk):
    def kernel(inverse_ref, shrunk_ref, out_ref, terms_ref):
        left = mixed(inverse_ref[:, :K], shrunk_ref[...])
        out_ref[...] = left
        high, middle, low = split3(left)
        terms_ref[...] = jnp.concatenate([high, high, middle, high, middle, low], axis=0).T

    return pl.pallas_call(
        kernel,
        out_shape=[
            jax.ShapeDtypeStruct((K, ROWS), F32),
            jax.ShapeDtypeStruct((ROWS, 6 * K), BF16),
        ],
        compiler_params=PARAMS,
        name="mix_left",
    )(inverse, shrunk)


def deflate(last, right_shrunk, left_terms, cross):
    def kernel(last_ref, shrunk_ref, left_ref, cross_ref, out_ref, right_ref, strength_ref, terms_ref):
        step = pl.program_id(0)

        @pl.when(step == 0)
        def _():
            packed = jnp.sum(last_ref[...], axis=0)
            last = jnp.concatenate([packed[:, : 2 * K], packed[:, 2 * K :]], axis=0)
            inverse = inverse_factor(last[:, :K], NG)
            right = mixed(inverse, shrunk_ref[...])
            right_ref[...] = right
            strength = jnp.sum(inverse * last[:, K:], axis=1, keepdims=True) / math.sqrt(NV * NG)
            strength_ref[...] = to_row(strength)[:, :K]
            high, middle, low = split3(right * (strength / math.sqrt(NV * NG)))
            terms_ref[...] = jnp.concatenate([high, middle, high, low, middle, high], axis=0)

        out_ref[...] = cross_ref[...] - dot(left_ref[...], terms_ref[...], NN)

    whole = lambda shape: pl.BlockSpec(shape, lambda i: (0,) * len(shape))
    return pl.pallas_call(
        kernel,
        grid=(ROWS // BLOCK,),
        in_specs=[
            whole((16, K // 2, LANES)),
            whole((K, COLS)),
            pl.BlockSpec((BLOCK, 6 * K), lambda i: (i, 0)),
            pl.BlockSpec((BLOCK, COLS), lambda i: (i, 0)),
        ],
        out_specs=[
            pl.BlockSpec((BLOCK, COLS), lambda i: (i, 0)),
            whole((K, COLS)),
            whole((1, K)),
        ],
        out_shape=[
            jax.ShapeDtypeStruct((ROWS, COLS), F32),
            jax.ShapeDtypeStruct((K, COLS), F32),
            jax.ShapeDtypeStruct((1, K), F32),
        ],
        scratch_shapes=[pltpu.VMEM((6 * K, COLS), BF16)],
        compiler_params=PARAMS,
        name="deflate",
    )(last, right_shrunk, left_terms, cross)


def per_device(cross, start, levels):
    for sweep in range(ITERS):
        if sweep == 0:
            *parts, cross, places = left_product_first(start, cross)
            got = [swap(parts[at + 1], "var", Z_RINGS, mask) for at, mask in enumerate(MASKS)]
            total = parts[0]
        else:
            *parts, both, gram = left_partners(right_sum, squares, levels, cross, places)
            got = [swap(part, "var", Z_RINGS, mask) for part, mask in zip(parts, MASKS)]
            total = left_own(both, gram, cross, places)
        total = (total + got[0]) + (got[1] + got[2])
        total = ring_sum(total, "var", Y_RINGS)
        block = total[:LEFT_ROWS]
        blocks = [block] + [swap(block, "var", Z_RINGS, mask) for mask in MASKS]
        inverse = factor(total[LEFT_ROWS:], NG) if sweep else None
        left_sum, squares = assemble(inverse, blocks, places, Z_AT, 1, "assemble_left")
        squares = ring_sum(pair_sum(squares), "vox", X_RINGS)

        part, both, gram, left_shrunk = right_half(True, (left_sum, squares, levels), cross, places, 1)
        got = swap(part, "vox", CORE_PAIRS, 1)
        (total,) = right_half(False, (both, gram), cross, places, 0)
        total = ring_sum(total + got, "vox", X_RINGS)
        block = total[:RIGHT_ROWS]
        got = swap(block, "vox", CORE_PAIRS, 1)
        inverse = factor(total[RIGHT_ROWS:], NV)
        if sweep == ITERS - 1:
            left_dirs, left_terms = mix_left(inverse, left_shrunk)
            got, left_terms = lax.optimization_barrier((got, left_terms))
        blocks = [block, got]
        right_sum, squares = assemble(inverse, blocks, places, CORE_AT, 16, "assemble_right")
        squares = from_all(squares)
    right_shrunk, last = last_shrink(right_sum, squares, levels)
    last = from_all(last)
    deflated, right_dirs, strength = deflate(last, right_shrunk, left_terms, cross)
    return (deflated, left_dirs, right_dirs, strength.reshape(K))


def solution(mesh):
    in_specs = (P("vox", "var"), P(None, "var"), P())
    out_specs = (P("vox", "var"), P(None, "vox"), P(None, "var"), P())
    return jax.shard_map(
        per_device, mesh=mesh, in_specs=in_specs, out_specs=out_specs, check_vma=False
    )
```
